32 devices in a mesh: wide: 8 (over z, y), narrow: 4 (over x, core).
Axes of the slice: x: 2, y: 2, z: 4, core: 2. Of those that a mesh axis runs over, the one named last changes fastest.
Arguments:
- tokens: bfloat16 [32, 1600], P('wide'), may hold values from -48 to 48
- source: int32 [32], P('wide'), may hold values from 0 to 31, each once
- lengths: int32 [32], P('wide'), may hold values from 1 to 4096
- cached_key_rows: bfloat16 [32, 1024, 320], P('wide', 'narrow'), may hold values from -160 to 160
- cached_value_rows: bfloat16 [32, 1024, 320], P('wide', 'narrow'), may hold values from -6 to 6
- conv_state: bfloat16 [32, 3, 1600], P('wide', None, 'narrow'), may hold values from -6 to 6
- ssm_state: float32 [32, 16, 1600], P('wide', None, 'narrow'), may hold values from -6 to 6
- norm_gain: float32 [1600], replicated, may hold values from 0.1 to 1.9
- query_key_value_weight: bfloat16 [1600, 2240], P(None, 'narrow'), may hold values from -0.15625 to 0.15625
- w_xz: bfloat16 [1600, 2, 1600], P(None, None, 'narrow'), may hold values from -0.15625 to 0.15625
- conv_weight: float32 [4, 1600], P(None, 'narrow'), may hold values from -3 to 3
- conv_bias: float32 [1600], P('narrow'), may hold values from -3 to 3
- w_xproj: bfloat16 [1600, 132], P('narrow'), may hold values from -0.15625 to 0.15625
- w_dt: bfloat16 [100, 1600], P(None, 'narrow'), may hold values from -0.625 to 0.625
- dt_bias: float32 [1600], P('narrow'), may hold values from -4 to 0.5
- a_log: float32 [16, 1600], P(None, 'narrow'), may hold values from 0 to 2.77
- skip_d: float32 [1600], P('narrow'), may hold values from 0.5 to 2
- w_attn_out: bfloat16 [1600, 1600], P(None, 'narrow'), may hold values from -0.15625 to 0.15625
- w_ssm_out: bfloat16 [1600, 1600], P('narrow'), may hold values from -0.15625 to 0.15625
- gain_attn: float32 [1600], P('narrow'), may hold values from 0.1 to 1.9
- gain_ssm: float32 [1600], P('narrow'), may hold values from 0.1 to 1.9
Outputs:
- out: bfloat16 [32, 1600], P('wide', 'narrow')
- new_kv: bfloat16 [32, 640], P('wide')
- new_conv: bfloat16 [32, 3, 1600], P('wide', None, 'narrow')
- new_ssm: float32 [32, 16, 1600], P('wide', None, 'narrow')
The draws below stay inside these ranges and needn't reach their ends.
Inputs may be any that keep to these rules, and one draw needn't show every extreme that they name: `source`: each of the 32 requests once.
All inputs are finite; a program needn't handle non-finite values.
Results may differ from the reference program's by a relative error of at most 0.005.
Values may be sent and summed in bfloat16 or wider, within the bound.
No kernel may reach another device: no remote copies, remote signals or barrier semaphores. Data moves between devices by JAX's collectives and lax.ppermute only.
A program may use at most 64 MiB of HBM per device.

```python
import math
import jax
import jax.numpy as jnp
from jax import lax

MODEL_WIDTH = 1600
QUERY_HEADS = 25
KEY_VALUE_HEADS = 5
HEAD_SIZE = 64
WINDOW_LENGTH = 1024
MI = 1600
NS = 16
KC = 4
DTR = 100
MAXLEN = 4096
REQUEST_SLOTS = 32


def draw_tokens(key, part):
    first = jax.random.fold_in(jax.random.fold_in(key, 3), 0)
    column_scale = jnp.exp(jnp.arange(MODEL_WIDTH, dtype=jnp.float32) * (math.log(3.0) / (MODEL_WIDTH - 1)))
    values = jnp.clip(jax.random.normal(first, (REQUEST_SLOTS, MODEL_WIDTH), jnp.float32), -5.0, 5.0)
    return (values * column_scale[None]).astype(jnp.bfloat16)


def draw_lengths(key, part):
    first, second, third, fourth = jax.random.split(jax.random.fold_in(key, 11), 4)
    long_length = jax.random.randint(first, (REQUEST_SLOTS,), 1, MAXLEN + 1)
    short_length = jax.random.randint(second, (REQUEST_SLOTS,), 1, WINDOW_LENGTH)
    picker = jax.random.randint(third, (REQUEST_SLOTS,), 0, 3)
    drawn = jnp.where(picker == 0, short_length, long_length)
    top_row = jax.random.randint(fourth, (), 0, REQUEST_SLOTS)
    return jnp.where(jnp.arange(REQUEST_SLOTS) == top_row, MAXLEN, drawn).astype(jnp.int32)


def draw_cached_key_rows(key, part):
    first = jax.random.fold_in(jax.random.fold_in(key, 17), 0)
    array_shape = (REQUEST_SLOTS, WINDOW_LENGTH, KEY_VALUE_HEADS * HEAD_SIZE)
    values = jnp.clip(jax.random.normal(first, array_shape, jnp.float32), -6.0, 6.0)
    return values.astype(jnp.bfloat16)


def level_of(rng, dims, pieces, least, top_value):
    level, own = 1.0, jax.random.fold_in(rng, 6)
    for dim, shards_of in pieces:
        draws = jnp.exp(jax.random.uniform(jax.random.fold_in(own, dim), (shards_of,), jnp.float32, least / len(pieces), top_value / len(pieces)))
        level = level * jnp.repeat(draws, dims[dim] // shards_of).reshape([-1 if axis == dim else 1 for axis in range(len(dims))])
    return level


def bell_draw(rng, shape, width, bound, shards=(), kind=jnp.bfloat16):
    values = jax.random.normal(rng, shape, jnp.float32) * width
    if len(shards) > 0:
        values = level_of(rng, shape, shards, -0.22, 0.18) * values
    return jnp.clip(values, min=-bound, max=bound).astype(kind)


def setup_inputs(seed: int = 0) -> dict:
    seeds = jax.random.split(jax.random.key(seed), 22)
    return {
        "tokens": draw_tokens(jax.random.fold_in(seeds[21], 71), 0),
        "source": jax.random.permutation(seeds[1], REQUEST_SLOTS).astype(jnp.int32),
        "lengths": draw_lengths(jax.random.fold_in(seeds[21], 71), 0),
        "cached_key_rows": draw_cached_key_rows(jax.random.fold_in(seeds[21], 71), 0),
        "cached_value_rows": bell_draw(seeds[4], (REQUEST_SLOTS, WINDOW_LENGTH, KEY_VALUE_HEADS * HEAD_SIZE), 1.0, 6.0, ((0, 8), (1, 4))),
        "conv_state": bell_draw(seeds[5], (REQUEST_SLOTS, KC - 1, MI), 1.0, 6.0, ((0, 8), (2, 4))),
        "ssm_state": bell_draw(seeds[6], (REQUEST_SLOTS, NS, MI), 1.0, 6.0, ((0, 8), (2, 4)), jnp.float32),
        "norm_gain": jnp.clip(1.0 + 0.18 * jax.random.normal(seeds[7], (MODEL_WIDTH,), jnp.float32), 0.1, 1.9),
        "query_key_value_weight": bell_draw(seeds[8], (MODEL_WIDTH, (QUERY_HEADS + 2 * KEY_VALUE_HEADS) * HEAD_SIZE), MODEL_WIDTH ** -0.5, 0.15625, ((1, 4),)),
        "w_xz": bell_draw(seeds[9], (MODEL_WIDTH, 2, MI), MODEL_WIDTH ** -0.5, 0.15625, ((2, 4),)),
        "conv_weight": bell_draw(seeds[10], (KC, MI), KC ** -0.5, 3.0, ((1, 4),), jnp.float32),
        "conv_bias": bell_draw(seeds[11], (MI,), 0.5, 3.0, ((0, 4),), jnp.float32),
        "w_xproj": bell_draw(seeds[12], (MI, DTR + 2 * NS), MI ** -0.5, 0.15625, ((0, 4),)),
        "w_dt": bell_draw(seeds[13], (DTR, MI), DTR ** -0.5, 0.625, ((1, 4),)),
        "dt_bias": jnp.clip(-4.0 + 4.5 * jax.random.uniform(seeds[14], (MI,), jnp.float32) ** level_of(seeds[14], (MI,), ((0, 4),), -0.2, 0.2), -4.0, 0.5),
        "a_log": jnp.clip(2.77 * jax.random.uniform(seeds[15], (NS, MI), jnp.float32) ** level_of(seeds[15], (NS, MI), ((1, 4),), -0.2, 0.2), 0.0, 2.77),
        "skip_d": jnp.clip(0.5 + 1.5 * jax.random.uniform(seeds[16], (MI,), jnp.float32) ** level_of(seeds[16], (MI,), ((0, 4),), -0.2, 0.2), 0.5, 2.0),
        "w_attn_out": bell_draw(seeds[17], (QUERY_HEADS * HEAD_SIZE, MODEL_WIDTH), (QUERY_HEADS * HEAD_SIZE) ** -0.5, 0.15625, ((1, 4),)),
        "w_ssm_out": bell_draw(seeds[18], (MI, MODEL_WIDTH), MI ** -0.5, 0.15625, ((0, 4),)),
        "gain_attn": jnp.clip(1.0 + 0.18 * jax.random.normal(seeds[19], (MODEL_WIDTH,), jnp.float32), 0.1, 1.9),
        "gain_ssm": jnp.clip(1.0 + 0.18 * jax.random.normal(seeds[20], (MODEL_WIDTH,), jnp.float32), 0.1, 1.9),
    }


EPSILON = 1e-06

def inverse_rms(values):
    return lax.rsqrt(lax.optimization_barrier(jnp.mean(values * values, axis=-1, keepdims=True)) + EPSILON)

def reference(tokens, source, lengths, cached_key_rows, cached_value_rows, conv_state, ssm_state, norm_gain, query_key_value_weight, w_xz, conv_weight, conv_bias, w_xproj, w_dt, dt_bias, a_log, skip_d, w_attn_out, w_ssm_out, gain_attn, gain_ssm):
    query_groups = QUERY_HEADS // KEY_VALUE_HEADS
    query_total_width = QUERY_HEADS * HEAD_SIZE
    key_value_width = KEY_VALUE_HEADS * HEAD_SIZE
    score_factor_scale = HEAD_SIZE ** (-0.5)
    routed = jnp.take(tokens, source, axis=0)
    routed_f = routed.astype(jnp.float32)
    normed = (routed_f * inverse_rms(routed_f) * norm_gain).astype(jnp.bfloat16)
    every_head = jnp.dot(normed, query_key_value_weight, preferred_element_type=jnp.float32).astype(jnp.bfloat16)
    new_kv = every_head[:, query_total_width:]
    both_parts = jnp.dot(normed, w_xz.reshape(MODEL_WIDTH, 2 * MI), preferred_element_type=jnp.float32).reshape(REQUEST_SLOTS, 2, MI)
    channel_in = both_parts[:, 0]
    gate_part = both_parts[:, 1]
    conv_out = conv_bias + lax.optimization_barrier(jnp.sum(conv_weight[:KC - 1][None] * conv_state.astype(jnp.float32), axis=1)) + conv_weight[KC - 1] * channel_in
    conv_act = jax.nn.silu(conv_out)
    new_conv = jnp.concatenate([conv_state[:, 1:], channel_in.astype(jnp.bfloat16)[:, None]], axis=1)
    state_inputs = jnp.dot(conv_act.astype(jnp.bfloat16), w_xproj, preferred_element_type=jnp.float32)
    step_low = state_inputs[:, :DTR]
    input_map = state_inputs[:, DTR:DTR + NS]
    output_map = state_inputs[:, DTR + NS:]
    step_size = jax.nn.softplus(jnp.dot(step_low.astype(jnp.bfloat16), w_dt, preferred_element_type=jnp.float32) + dt_bias)
    decay = jnp.exp(-step_size[:, None, :] * jnp.exp(a_log)[None])
    new_ssm = decay * ssm_state + step_size[:, None, :] * input_map[:, :, None] * conv_act[:, None, :]
    state_out = lax.optimization_barrier(jnp.sum(output_map[:, :, None] * new_ssm, axis=1)) + skip_d * conv_act
    ssm_heads = (state_out * jax.nn.silu(gate_part)).astype(jnp.bfloat16)

    def attend(packed):
        query_vector, current_key, current_value, window_keys, window_values, length = packed
        query_vector = query_vector.reshape(KEY_VALUE_HEADS, query_groups, HEAD_SIZE).astype(jnp.float32)
        key_float = window_keys.reshape(WINDOW_LENGTH, KEY_VALUE_HEADS, HEAD_SIZE).astype(jnp.float32)
        value_float = window_values.reshape(WINDOW_LENGTH, KEY_VALUE_HEADS, HEAD_SIZE).astype(jnp.float32)
        score = jnp.einsum('gjd,tgd->gjt', query_vector, key_float) * score_factor_scale
        current_score = jnp.einsum('wpx,wx->wp', query_vector, current_key.reshape(KEY_VALUE_HEADS, HEAD_SIZE).astype(jnp.float32)) * score_factor_scale
        slot_index = jnp.arange(WINDOW_LENGTH, dtype=jnp.int32)
        live = (slot_index < length) & jnp.logical_not((length >= WINDOW_LENGTH) & (slot_index == length % WINDOW_LENGTH))
        score_top = jnp.maximum(lax.optimization_barrier(jnp.max(jnp.where(live, score, -jnp.inf), axis=2)), current_score)
        weights = jnp.where(live, jnp.exp(score - score_top[:, :, None]), 0.0).astype(jnp.bfloat16)
        current_weight = jnp.exp(current_score - score_top).astype(jnp.bfloat16).astype(jnp.float32)
        weight_float = weights.astype(jnp.float32)
        weighted_numer = jnp.einsum('acs,say->acy', weight_float, value_float) + current_weight[:, :, None] * current_value.reshape(KEY_VALUE_HEADS, HEAD_SIZE).astype(jnp.float32)[:, None, :]
        denominator = lax.optimization_barrier(jnp.sum(weight_float, axis=2)) + current_weight
        return (weighted_numer / denominator[:, :, None]).reshape(query_total_width).astype(jnp.bfloat16)
    attn_heads = lax.map(attend, (every_head[:, :query_total_width], every_head[:, query_total_width:query_total_width + key_value_width], every_head[:, query_total_width + key_value_width:], cached_key_rows, cached_value_rows, lengths))
    y_attn = jnp.dot(attn_heads, w_attn_out, preferred_element_type=jnp.float32)
    y_ssm = jnp.dot(ssm_heads, w_ssm_out, preferred_element_type=jnp.float32)
    mixed = 0.5 * (y_attn * inverse_rms(y_attn) * gain_attn + y_ssm * inverse_rms(y_ssm) * gain_ssm)
    out = (routed_f + mixed).astype(jnp.bfloat16)
    return (out, new_kv, new_conv, new_ssm)
```

```python
import jax
import jax.numpy as jnp
from jax import lax
from jax.sharding import PartitionSpec as P

MODEL_WIDTH = 1600
QUERY_HEADS = 25
KEY_VALUE_HEADS = 5
HEAD_SIZE = 64
WINDOW_LENGTH = 1024


EPSILON = 1e-06


def exchange(part, axis):
    size = lax.axis_size(axis)
    me = lax.axis_index(axis)
    pieces = [part] + [
        lax.ppermute(part, axis, [(i, (i + step) % size) for i in range(size)])
        for step in range(1, size)
    ]
    stacked = jnp.stack(pieces)
    return jnp.take(stacked, (me - jnp.arange(size)) % size, axis=0, mode="clip")


def exchange_sum(part, axis):
    size = lax.axis_size(axis)
    total = part
    for step in range(1, size):
        total = total + lax.ppermute(part, axis, [(i, (i + step) % size) for i in range(size)])
    return total


def shards(
    tokens,
    source,
    lengths,
    cached_key_rows,
    cached_value_rows,
    conv_state,
    ssm_state,
    norm_gain,
    query_key_value_weight,
    w_xz,
    conv_weight,
    conv_bias,
    w_xproj,
    w_dt,
    dt_bias,
    a_log,
    skip_d,
    w_attn_out,
    w_ssm_out,
    gain_attn,
    gain_ssm,
):
    query_groups = QUERY_HEADS // KEY_VALUE_HEADS
    query_total_width = QUERY_HEADS * HEAD_SIZE
    key_value_width = KEY_VALUE_HEADS * HEAD_SIZE
    score_factor_scale = HEAD_SIZE ** (-0.5)
    rows = tokens.shape[0]
    wide = lax.axis_size("wide")
    narrow = lax.axis_size("narrow")
    me = lax.axis_index("narrow")
    col_width = MODEL_WIDTH // narrow
    col_start = me * col_width

    arrived = lax.all_to_all(jnp.broadcast_to(tokens[None], (wide,) + tokens.shape), "wide", 0, 0)
    arrived = arrived.reshape(wide * rows, MODEL_WIDTH)
    routed_full = jnp.take(arrived, source, axis=0, mode="clip").astype(jnp.float32)
    row_scale = lax.rsqrt(jnp.mean(routed_full * routed_full, axis=1) + EPSILON)
    normed = (routed_full * row_scale[:, None] * norm_gain).astype(jnp.bfloat16)
    routed_cols = lax.dynamic_slice_in_dim(routed_full, col_start, col_width, 1)
    head_part = jnp.dot(normed, query_key_value_weight, preferred_element_type=jnp.float32).astype(
        jnp.bfloat16
    )
    inner_weights = w_xz.reshape(w_xz.shape[0], -1)
    both_parts = jnp.dot(normed, inner_weights, preferred_element_type=jnp.float32).reshape(
        rows, 2, -1
    )
    channel_in = both_parts[:, 0]
    gate_part = both_parts[:, 1]
    conv_out = (
        conv_bias
        + jnp.sum(conv_weight[:-1][None] * conv_state.astype(jnp.float32), axis=1)
        + conv_weight[-1] * channel_in
    )
    conv_act = jax.nn.silu(conv_out)
    new_conv = jnp.concatenate(
        [conv_state[:, 1:], channel_in.astype(jnp.bfloat16)[:, None]], axis=1
    )
    state_part = jnp.dot(conv_act.astype(jnp.bfloat16), w_xproj, preferred_element_type=jnp.float32)

    head_width = head_part.shape[1]
    first = exchange(jnp.concatenate([head_part.astype(jnp.float32), state_part], axis=1), "narrow")
    every_head = (
        first[:, :, :head_width].transpose(1, 0, 2).reshape(rows, -1).astype(jnp.bfloat16)
    )
    new_kv = every_head[:, query_total_width:]
    state_inputs = jnp.sum(first[:, :, head_width:], axis=0)

    rank_width = w_dt.shape[0]
    state_width = (state_inputs.shape[1] - rank_width) // 2
    step_low = state_inputs[:, :rank_width]
    input_map = state_inputs[:, rank_width : rank_width + state_width]
    output_map = state_inputs[:, rank_width + state_width :]
    step_size = jax.nn.softplus(
        jnp.dot(step_low.astype(jnp.bfloat16), w_dt, preferred_element_type=jnp.float32) + dt_bias
    )
    decay_rate = jnp.exp(-step_size[:, None, :] * jnp.exp(a_log)[None])
    new_ssm = (
        decay_rate * ssm_state
        + step_size[:, None, :] * input_map[:, :, None] * conv_act[:, None, :]
    )
    state_out = jnp.sum(output_map[:, :, None] * new_ssm, axis=1) + skip_d * conv_act
    ssm_heads = (state_out * jax.nn.silu(gate_part)).astype(jnp.bfloat16)
    state_partial = jnp.dot(ssm_heads, w_ssm_out, preferred_element_type=jnp.float32)

    request_slot_count = cached_key_rows.shape[1]
    slot_index = me * request_slot_count + lax.iota(jnp.int32, request_slot_count)
    length_col = lengths[:, None]
    live_slots = (slot_index[None] < length_col) & jnp.logical_not(
        (length_col >= WINDOW_LENGTH) & (slot_index[None] == length_col % WINDOW_LENGTH)
    )
    live_mask = live_slots[:, None, None, :]
    query_rows = every_head[:, :query_total_width].reshape(
        rows, KEY_VALUE_HEADS, query_groups, HEAD_SIZE
    )
    current_key = every_head[:, query_total_width : query_total_width + key_value_width].reshape(
        rows, KEY_VALUE_HEADS, HEAD_SIZE
    )
    current_value = every_head[:, query_total_width + key_value_width :].reshape(
        rows, KEY_VALUE_HEADS, HEAD_SIZE
    )
    window_keys = cached_key_rows.reshape(rows, request_slot_count, KEY_VALUE_HEADS, HEAD_SIZE)
    window_values = cached_value_rows.reshape(rows, request_slot_count, KEY_VALUE_HEADS, HEAD_SIZE)
    score_all = (
        jnp.einsum("rgjd,rtgd->rgjt", query_rows, window_keys, preferred_element_type=jnp.float32)
        * score_factor_scale
    )
    current_score = (
        jnp.einsum("rgjd,rgd->rgj", query_rows, current_key, preferred_element_type=jnp.float32)
        * score_factor_scale
    )
    local_top = jnp.maximum(
        jnp.max(jnp.where(live_mask, score_all, -jnp.inf), axis=3), current_score
    )
    weights = jnp.where(live_mask, jnp.exp(score_all - local_top[..., None]), 0.0).astype(
        jnp.bfloat16
    )
    numer = jnp.einsum(
        "rgjt,rtgd->rgjd", weights, window_values, preferred_element_type=jnp.float32
    ).reshape(rows, query_total_width)
    denom = jnp.sum(weights.astype(jnp.float32), axis=3).reshape(rows, QUERY_HEADS)

    second = exchange(
        jnp.concatenate([numer, state_partial, local_top.reshape(rows, -1), denom], axis=1),
        "narrow",
    )
    numers = second[:, :, :query_total_width]
    y_ssm = jnp.sum(second[:, :, query_total_width : query_total_width + MODEL_WIDTH], axis=0)
    stats = second[:, :, query_total_width + MODEL_WIDTH :]
    tops, denoms = stats[:, :, :QUERY_HEADS], stats[:, :, QUERY_HEADS:]
    top = jnp.max(tops, axis=0)
    factor = jnp.exp(tops - top[None])
    own = jnp.exp(current_score.reshape(rows, -1) - top).astype(jnp.bfloat16).astype(jnp.float32)
    total_den = jnp.sum(factor * denoms, axis=0) + own
    total_num = jnp.sum(
        factor[..., None] * numers.reshape(narrow, rows, QUERY_HEADS, HEAD_SIZE), axis=0
    ) + own[..., None] * jnp.repeat(current_value.astype(jnp.float32), query_groups, axis=1)
    attn_heads = (
        (total_num / total_den[..., None]).reshape(rows, query_total_width).astype(jnp.bfloat16)
    )
    y_attn = jnp.dot(attn_heads, w_attn_out, preferred_element_type=jnp.float32)

    attn_square = exchange_sum(jnp.sum(y_attn * y_attn, axis=1), "narrow")
    attn_scale = lax.rsqrt(attn_square / MODEL_WIDTH + EPSILON)
    state_scale = lax.rsqrt(jnp.mean(y_ssm * y_ssm, axis=1) + EPSILON)
    y_ssm_cols = lax.dynamic_slice_in_dim(y_ssm, col_start, col_width, 1)
    mixed = 0.5 * (
        y_attn * attn_scale[:, None] * gain_attn + y_ssm_cols * state_scale[:, None] * gain_ssm
    )
    out = (routed_cols + mixed).astype(jnp.bfloat16)
    return (out, new_kv, new_conv, new_ssm)


def solution(mesh):
    placed = (
        P("wide", None),
        P("wide"),
        P("wide"),
        P("wide", "narrow", None),
        P("wide", "narrow", None),
        P("wide", None, "narrow"),
        P("wide", None, "narrow"),
        P(),
        P(None, "narrow"),
        P(None, None, "narrow"),
        P(None, "narrow"),
        P("narrow"),
        P("narrow", None),
        P(None, "narrow"),
        P("narrow"),
        P(None, "narrow"),
        P("narrow"),
        P(None, "narrow"),
        P("narrow", None),
        P("narrow"),
        P("narrow"),
    )
    return jax.shard_map(
        shards,
        mesh=mesh,
        in_specs=placed,
        out_specs=(
            P("wide", "narrow"),
            P("wide", None),
            P("wide", None, "narrow"),
            P("wide", None, "narrow"),
        ),
        check_vma=False,
    )
```

```python
import functools
import jax
import jax.numpy as jnp
from jax import lax
from jax.experimental import pallas as pl
from jax.experimental.pallas import tpu as pltpu
from jax.sharding import PartitionSpec as P

MODEL_WIDTH = 1600
QUERY_HEADS = 25
KEY_VALUE_HEADS = 5
HEAD_SIZE = 64
WINDOW_LENGTH = 1024
GROUP = QUERY_HEADS // KEY_VALUE_HEADS
QUERY_WIDTH = QUERY_HEADS * HEAD_SIZE
KEY_VALUE_WIDTH = KEY_VALUE_HEADS * HEAD_SIZE


EPSILON = 1e-06

NT = (((1,), (1,)), ((), ()))
F32 = jnp.float32
BF16 = jnp.bfloat16


def dot_nt(a, b):
    return lax.dot_general(a, b, NT, preferred_element_type=F32)


def sigmoid(v):
    return 1.0 / (1.0 + jnp.exp(-v))


def exchange(part, axis):
    size = lax.axis_size(axis)
    return [part] + [
        lax.ppermute(part, axis, [(i, (i + step) % size) for i in range(size)])
        for step in range(1, size)
    ]


def gather_xor(part, axis):
    size = lax.axis_size(axis)
    assert size & (size - 1) == 0
    digits = size.bit_length() - 1
    blocks = [part[None]]
    done = 0
    while done < digits:
        held = blocks[0] if len(blocks) == 1 else jnp.concatenate(blocks)
        wide = 1 if (digits - done) % 2 else 2
        blocks = [held] + [
            lax.ppermute(held, axis, [(i, i ^ (step << done)) for i in range(size)])
            for step in range(1, 1 << wide)
        ]
        done += wide
    return blocks


def stack_pieces(me, pieces, held):
    size = len(pieces)
    for step, piece in enumerate(pieces):
        held[lax.rem(me - step + size, size)] = piece[...]


def prepare(place_ref, source_ref, *refs, count):
    rows = source_ref.shape[0]
    given, (chosen_ref, base_ref, new_conv_ref, *kept), (conv_w, conv_b, conv_rows, sems) = (
        refs[: count + 3], refs[count + 3 : -4], refs[-4:])
    large, small = given[:count], given[count:]
    copies = [
        pltpu.make_async_copy(origin, to, sems.at[i])
        for i, (origin, to) in enumerate(zip((*small, *large), (conv_w, conv_b, conv_rows, *kept)))
    ]
    for copy in copies:
        copy.start()
    slots = chosen_ref.shape[1]
    row_id = lax.broadcasted_iota(jnp.int32, (8, slots), 0)
    wanted = jnp.full((8, slots), -1, jnp.int32)
    for r in range(rows):
        origin = lax.bitwise_xor(lax.div(source_ref[r], rows), place_ref[0])
        wanted = jnp.where(row_id == r, origin * rows + lax.rem(source_ref[r], rows), wanted)
    chosen = lax.broadcasted_iota(jnp.int32, (8, slots), 1) == wanted
    chosen_ref[...] = jnp.where(chosen, 1.0, 0.0)
    for copy in copies[:3]:
        copy.wait()
    taps = conv_rows.shape[0]
    base = conv_b[...]
    for tap in range(taps):
        base = base + conv_w[tap : tap + 1] * conv_rows[tap].astype(F32)
    base_ref[:rows] = base
    base_ref[rows:] = jnp.broadcast_to(conv_w[taps:], base.shape)
    for tap in range(taps - 1):
        new_conv_ref[tap] = conv_rows[tap + 1]
    new_conv_ref[taps - 1] = jnp.zeros_like(conv_rows[0])
    for copy in copies[3:]:
        copy.wait()


def project_in(me_ref, *refs, size):
    arrived_refs = refs[:size]
    (chosen_ref, base_ref, old_conv_ref, gain_ref, heads_w_ref, xz_w_ref, xproj_ref, part_ref,
     act_ref, gate_ref, new_conv_ref, cols_ref, blocks) = refs[size:]
    rows, cols = cols_ref.shape
    arrived = jnp.concatenate(
        [ref[i].astype(F32) for ref in arrived_refs for i in range(ref.shape[0])], axis=0
    ).astype(BF16)
    routed = jnp.dot(chosen_ref[...].astype(BF16), arrived, preferred_element_type=F32)
    for block in range(blocks.shape[0]):
        blocks[block] = routed[:rows, block * cols : (block + 1) * cols]
    cols_ref[...] = blocks[me_ref[0]]
    scale = lax.rsqrt(jnp.mean(routed * routed, axis=1, keepdims=True) + EPSILON)
    normed = (routed * scale * gain_ref[...]).astype(BF16)
    heads = dot_nt(normed, heads_w_ref[...])[:rows].astype(BF16).astype(F32)
    channel_in = dot_nt(normed, xz_w_ref[0])[:rows]
    gate = dot_nt(normed, xz_w_ref[1])[:rows]
    taps = old_conv_ref.shape[0]
    conv_out = base_ref[:rows] + base_ref[rows:] * channel_in
    act = conv_out * sigmoid(conv_out)
    for tap in range(taps - 1):
        new_conv_ref[tap] = old_conv_ref[tap]
    new_conv_ref[taps - 1] = channel_in.astype(BF16)
    act_ref[...] = act
    gate_ref[...] = gate * sigmoid(gate)
    state = dot_nt(act.astype(BF16), xproj_ref[...])
    part_ref[...] = jnp.concatenate([heads, state], axis=1)


def mix(
    me_ref, lengths_ref, *refs, size, head_width,
):
    pieces = refs[:size]
    (keys_ref, values_ref, act_ref, gate_ref, dt_w_ref, dt_b_ref, a_log_ref, ssm_ref, skip_ref,
     out_w_ref, part_ref, new_ssm_ref, new_kv_ref, held) = refs[size:]
    me = me_ref[0]
    stack_pieces(me, pieces, held)
    rows = held.shape[1]
    heads = jnp.concatenate([held[i][:, :head_width] for i in range(size)], axis=1)
    state = held[0][:, head_width:]
    for i in range(1, size):
        state = state + held[i][:, head_width:]
    new_kv_ref[...] = heads[:, QUERY_WIDTH:].astype(BF16)

    rank = dt_w_ref.shape[1]
    depth = a_log_ref.shape[0]
    step = dot_nt(state[:, :rank].astype(BF16), dt_w_ref[...]) + dt_b_ref[...]
    step = jnp.maximum(step, 0.0) + jnp.log1p(jnp.exp(-jnp.abs(step)))
    act = act_ref[...]
    rates = jnp.exp(a_log_ref[...])
    maps = jnp.concatenate(
        [state[:, rank:], jnp.zeros((rows, 128 - 2 * depth), F32)], axis=1
    )
    maps = jnp.concatenate([maps, jnp.zeros((8 - rows, 128), F32)], axis=0).T
    outs = []
    for r in range(rows):
        step_row = step[r : r + 1]
        fresh = jnp.exp(-step_row * rates) * ssm_ref[r] + maps[:depth, r : r + 1] * (
            step_row * act[r : r + 1]
        )
        new_ssm_ref[r] = fresh
        outs.append(jnp.sum(maps[depth : 2 * depth, r : r + 1] * fresh, axis=0, keepdims=True))
    state_out = jnp.concatenate(outs, axis=0) + skip_ref[...] * act
    ssm_heads = (state_out * gate_ref[...]).astype(BF16)
    y_part = jnp.dot(ssm_heads, out_w_ref[...], preferred_element_type=F32)

    span = keys_ref.shape[2]
    tall = jnp.concatenate([heads, jnp.zeros((8 - rows, heads.shape[1]), F32)], axis=0)
    row_id = lax.broadcasted_iota(jnp.int32, (8, span), 0)
    slot = lax.broadcasted_iota(jnp.int32, (8, span), 1) + me * span
    length = jnp.zeros((8, span), jnp.int32)
    hole = jnp.zeros((8, span), jnp.int32)
    for r in range(rows):
        count = lengths_ref[r]
        length = jnp.where(row_id == r, count, length)
        hole = jnp.where(
            row_id == r, jnp.where(count >= WINDOW_LENGTH, lax.rem(count, WINDOW_LENGTH), -1), hole
        )
    live = (slot < length) & (slot != hole)
    live = jnp.concatenate([live.astype(F32)] * GROUP, axis=0) > 0.0
    tile_row = lax.rem(lax.broadcasted_iota(jnp.int32, (8 * GROUP, 1), 0), 8)
    own_here = jnp.where(me == 0, 1.0, 0.0)
    numers, tops, totals = [], [], []
    for g in range(KEY_VALUE_HEADS):
        at = QUERY_WIDTH + g * HEAD_SIZE
        new_key = tall[:, at : at + HEAD_SIZE]
        new_value = tall[:, at + KEY_VALUE_WIDTH : at + KEY_VALUE_WIDTH + HEAD_SIZE]
        queries = jnp.concatenate(
            [
                tall[:, j * HEAD_SIZE : (j + 1) * HEAD_SIZE]
                for j in range(g * GROUP, (g + 1) * GROUP)
            ],
            axis=0,
        ) * (HEAD_SIZE ** -0.5)
        own = jnp.sum(queries * jnp.concatenate([new_key] * GROUP, axis=0), axis=1, keepdims=True)
        packed = queries.astype(BF16)
        score = jnp.zeros((8 * GROUP, span), F32)
        for r in range(rows):
            one = jnp.dot(
                packed,
                keys_ref[r, g * HEAD_SIZE : (g + 1) * HEAD_SIZE, :],
                preferred_element_type=F32,
            )
            score = jnp.where(tile_row == r, one, score)
        top = jnp.maximum(
            jnp.max(jnp.where(live, score, -jnp.inf), axis=1, keepdims=True), own
        )
        weight = jnp.where(live, jnp.exp(score - top), 0.0).astype(BF16)
        own_weight = jnp.exp(own - top).astype(BF16).astype(F32) * own_here
        total = jnp.sum(weight.astype(F32), axis=1, keepdims=True) + own_weight
        numer = jnp.zeros((8 * GROUP, HEAD_SIZE), F32)
        for r in range(rows):
            one = dot_nt(weight, values_ref[r, g * HEAD_SIZE : (g + 1) * HEAD_SIZE, :])
            numer = jnp.where(tile_row == r, one, numer)
        numer = numer + own_weight * jnp.concatenate([new_value] * GROUP, axis=0)
        for j in range(GROUP):
            numers.append(numer[8 * j : 8 * j + 8])
            tops.append(top[8 * j : 8 * j + 8])
            totals.append(total[8 * j : 8 * j + 8])
    line = jnp.concatenate(numers + tops + totals, axis=1)[:rows]
    part_ref[:, : line.shape[1]] = line
    part_ref[:, line.shape[1] :] = y_part


def project_out(
    me_ref, *refs, size,
):
    pieces = refs[:size]
    (spread_ref, w_ref, cols_ref, gain_ref, y_ref, base_ref, square_ref, blocks) = refs[size:]
    rows = cols_ref.shape[0]
    cols = cols_ref.shape[1]
    lows = QUERY_WIDTH
    tops = [p[:, lows : lows + QUERY_HEADS] for p in pieces]
    totals = [p[:, lows + QUERY_HEADS : lows + 2 * QUERY_HEADS] for p in pieces]
    top = functools.reduce(jnp.maximum, tops)
    factors = [jnp.exp(t - top) for t in tops]
    total = functools.reduce(jnp.add, [f * t for f, t in zip(factors, totals)])
    factors = jnp.concatenate([f / total for f in factors], axis=0)
    high = factors.astype(BF16)
    low = (factors - high.astype(F32)).astype(BF16)
    spread = jnp.dot(high, spread_ref[...], preferred_element_type=F32) + jnp.dot(
        low, spread_ref[...], preferred_element_type=F32
    )
    merged = functools.reduce(
        jnp.add,
        [spread[i * rows : (i + 1) * rows] * p[:, :QUERY_WIDTH] for i, p in enumerate(pieces)],
    )
    y_attn = dot_nt(merged.astype(BF16), w_ref[...])
    y_ref[...] = y_attn
    square_ref[...] = jnp.broadcast_to(
        jnp.sum(y_attn * y_attn, axis=1, keepdims=True), square_ref.shape
    )
    lows = lows + 2 * QUERY_HEADS
    y_ssm = functools.reduce(jnp.add, [p[:, lows : lows + MODEL_WIDTH] for p in pieces])
    scale = lax.rsqrt(jnp.mean(y_ssm * y_ssm, axis=1, keepdims=True) + EPSILON)
    for block in range(blocks.shape[0]):
        blocks[block] = y_ssm[:, block * cols : (block + 1) * cols]
    base_ref[...] = cols_ref[...] + 0.5 * (blocks[me_ref[0]] * scale * gain_ref[...])


def finish(*refs, size):
    squares = refs[:size]
    y_ref, base_ref, gain_ref, out_ref = refs[size:]
    square = functools.reduce(jnp.add, [s[:, :1] for s in squares])
    scale = lax.rsqrt(square / MODEL_WIDTH + EPSILON)
    out_ref[...] = (base_ref[...] + 0.5 * (y_ref[...] * scale * gain_ref[...])).astype(BF16)


SMEM = pl.BlockSpec(memory_space=pltpu.SMEM)
VMEM = pl.BlockSpec(memory_space=pltpu.VMEM)


def call(body, scalars, blocks, outs, scratch=()):
    return pl.pallas_call(
        body,
        in_specs=[SMEM] * len(scalars) + [VMEM] * len(blocks),
        out_specs=[VMEM] * len(outs),
        out_shape=outs,
        scratch_shapes=scratch,
        compiler_params=pltpu.CompilerParams(vmem_limit_bytes=16 * 1024 * 1024),
    )(*scalars, *blocks)


def shards(
    tokens,
    source,
    lengths,
    cached_key_rows,
    cached_value_rows,
    conv_state,
    ssm_state,
    norm_gain,
    query_key_value_weight,
    w_xz,
    conv_weight,
    conv_bias,
    w_xproj,
    w_dt,
    dt_bias,
    a_log,
    skip_d,
    w_attn_out,
    w_ssm_out,
    gain_attn,
    gain_ssm,
):
    rows = tokens.shape[0]
    narrow = lax.axis_size("narrow")
    me = lax.axis_index("narrow").astype(jnp.int32).reshape(1)
    cols = MODEL_WIDTH // narrow
    head_width = query_key_value_weight.shape[1]
    shape = jax.ShapeDtypeStruct

    place = lax.axis_index("wide").astype(jnp.int32).reshape(1)
    arrived = gather_xor(tokens, "wide")

    large = (
        norm_gain[None], query_key_value_weight.T, w_xz.transpose(1, 2, 0), w_xproj.T,
    )
    small = (conv_weight, conv_bias[None], conv_state.transpose(1, 0, 2))
    slots = rows * lax.axis_size("wide")
    anywhere = pl.BlockSpec(memory_space=pl.ANY)
    prepared = pl.pallas_call(
        functools.partial(prepare, count=len(large)),
        in_specs=[SMEM] * 2 + [anywhere] * (len(large) + len(small)),
        out_specs=[VMEM] * (3 + len(large)),
        out_shape=[
            pltpu.VMEM((8, slots), F32),
            pltpu.VMEM((2 * rows, cols), F32),
            pltpu.VMEM(small[2].shape, BF16),
            *(pltpu.VMEM(a.shape, a.dtype) for a in large),
        ],
        scratch_shapes=[pltpu.VMEM(a.shape, a.dtype) for a in small]
        + [pltpu.SemaphoreType.DMA((len(large) + len(small),))],
        compiler_params=pltpu.CompilerParams(vmem_limit_bytes=4 * 1024 * 1024),
        cost_estimate=pl.CostEstimate(
            flops=0, transcendentals=0, bytes_accessed=2 * sum(a.size * a.dtype.itemsize for a in large)
        ),
    )(place, source, *(pltpu.with_memory_space_constraint(a, pltpu.HBM) for a in large + small))
    part_width = head_width + w_xproj.shape[1]
    part, act, gate, new_conv, routed_cols = call(
        functools.partial(project_in, size=len(arrived)),
        (me,),
        (*arrived, *prepared),
        (
            shape((rows, part_width), F32),
            shape((rows, cols), F32),
            shape((rows, cols), F32),
            shape((conv_state.shape[1], rows, cols), BF16),
            shape((rows, cols), F32),
        ),
        (pltpu.VMEM((narrow, rows, cols), F32),),
    )
    pieces = exchange(part, "narrow")
    second_width = QUERY_WIDTH + 2 * QUERY_HEADS + MODEL_WIDTH
    part, new_ssm, new_kv = call(
        functools.partial(mix, size=narrow, head_width=head_width),
        (me, lengths),
        (
            *pieces,
            cached_key_rows.transpose(0, 2, 1),
            cached_value_rows.transpose(0, 2, 1),
            act,
            gate,
            w_dt.T,
            dt_bias[None],
            a_log,
            ssm_state,
            skip_d[None],
            w_ssm_out,
        ),
        (
            shape((rows, second_width), F32),
            shape(ssm_state.shape, F32),
            shape((rows, 2 * KEY_VALUE_WIDTH), BF16),
        ),
        (pltpu.VMEM((narrow, rows, part_width), F32),),
    )
    pieces = exchange(part, "narrow")
    spread = (
        lax.broadcasted_iota(jnp.int32, (QUERY_HEADS, QUERY_WIDTH), 1) // HEAD_SIZE
        == lax.broadcasted_iota(jnp.int32, (QUERY_HEADS, QUERY_WIDTH), 0)
    ).astype(BF16)
    y_attn, base, square = call(
        functools.partial(project_out, size=narrow),
        (me,),
        (*pieces, spread, w_attn_out.T, routed_cols, gain_ssm[None]),
        (
            shape((rows, cols), F32),
            shape((rows, cols), F32),
            shape((rows, 128), F32),
        ),
        (pltpu.VMEM((narrow, rows, cols), F32),),
    )
    squares = exchange(square, "narrow")
    (out,) = call(
        functools.partial(finish, size=narrow),
        (),
        (*squares, y_attn, base, gain_attn[None]),
        (shape((rows, cols), BF16),),
    )
    return (out, new_kv, new_conv.transpose(1, 0, 2), new_ssm)


def solution(mesh):
    placed = (
        P("wide", None),
        P("wide"),
        P("wide"),
        P("wide", "narrow", None),
        P("wide", "narrow", None),
        P("wide", None, "narrow"),
        P("wide", None, "narrow"),
        P(),
        P(None, "narrow"),
        P(None, None, "narrow"),
        P(None, "narrow"),
        P("narrow"),
        P("narrow", None),
        P(None, "narrow"),
        P("narrow"),
        P(None, "narrow"),
        P("narrow"),
        P(None, "narrow"),
        P("narrow", None),
        P("narrow"),
        P("narrow"),
    )
    return jax.shard_map(
        shards,
        mesh=mesh,
        in_specs=placed,
        out_specs=(
            P("wide", "narrow"),
            P("wide", None),
            P("wide", None, "narrow"),
            P("wide", None, "narrow"),
        ),
        check_vma=False,
    )
```

```python
import functools
import jax
import jax.numpy as jnp
from jax import lax
from jax.experimental import pallas as pl
from jax.experimental.pallas import tpu as pltpu
from jax.sharding import PartitionSpec as P

MODEL_WIDTH = 1600
QUERY_HEADS = 25
KEY_VALUE_HEADS = 5
HEAD_SIZE = 64
WINDOW_LENGTH = 1024
GROUP = QUERY_HEADS // KEY_VALUE_HEADS
QUERY_WIDTH = QUERY_HEADS * HEAD_SIZE
KEY_VALUE_WIDTH = KEY_VALUE_HEADS * HEAD_SIZE


EPSILON = 1e-06
PARTS = 4

NT = (((1,), (1,)), ((), ()))
F32 = jnp.float32
BF16 = jnp.bfloat16


def dot_nt(a, b):
    return lax.dot_general(a, b, NT, preferred_element_type=F32)


def sigmoid(v):
    return 1.0 / (1.0 + jnp.exp(-v))


def exchange(part, axis):
    size = lax.axis_size(axis)
    return [part] + [
        lax.ppermute(part, axis, [(i, (i + step) % size) for i in range(size)])
        for step in range(1, size)
    ]


def join(*refs):
    *given, out_ref = refs
    at = 0
    for ref in given:
        if ref.shape[1:] == out_ref.shape[1:]:
            out_ref[at : at + ref.shape[0]] = ref[...]
            at += ref.shape[0]


def digits_of(size):
    assert size & (size - 1) == 0
    rounds, done, total = [], 0, size.bit_length() - 1
    while done < total:
        count = 1 if (total - done) % 2 else 2
        rounds.append((done, count))
        done += count
    return rounds


def gather_xor(part, axis, beside):
    size = lax.axis_size(axis)
    blocks = [part[None]]
    for place, count in digits_of(size):
        held = blocks[0]
        if len(blocks) > 1:
            entries = sum(b.shape[0] for b in blocks)
            (held,) = call(
                join, (), (*blocks, *beside), (jax.ShapeDtypeStruct((entries, *part.shape), part.dtype),)
            )
            beside = ()
        blocks = [held] + [
            lax.ppermute(held, axis, [(i, i ^ (step << place)) for i in range(size)])
            for step in range((1 << count) - 1, 0, -1)
        ]
    return blocks


def entry_of(away, size):
    entry = jnp.int32(0)
    for place, count in digits_of(size):
        top = (1 << count) - 1
        digit = lax.bitwise_and(lax.shift_right_logical(away, place), top)
        entry = entry + lax.shift_left(lax.bitwise_and(top + 1 - digit, top), place)
    return entry


def stack_pieces(me, pieces, held):
    size = len(pieces)
    for step, piece in enumerate(pieces):
        held[lax.rem(me - step + size, size)] = piece[...]


def cut(rows, count):
    step = -(-rows // (16 * count)) * 16
    return [(at, min(step, rows - at)) for at in range(0, rows, step)]


def copies_of(pairs, sems):
    copies = []
    for origin, to in pairs:
        if len(to.shape) == 2 and to.shape[0] >= 256:
            ranges = [pl.ds(at, size) for at, size in cut(to.shape[0], PARTS)]
            copies += [(origin.at[r], to.at[r]) for r in ranges]
        else:
            copies.append((origin, to))
    return [pltpu.make_async_copy(origin, to, sems.at[i]) for i, (origin, to) in enumerate(copies)]


def prepare(
    place_ref, source_ref, gain_ref, conv_w_ref, conv_b_ref, conv_rows_ref, heads_ref, xproj_ref, xz_ref,
    chosen_ref, base_ref, new_conv_ref, gain_out, heads_out, xproj_out, in_out,
    source, gain, conv_w, conv_b, conv_rows, sems,
):
    rows = source.shape[0]
    small = (
        (source_ref, source), (gain_ref, gain), (conv_w_ref, conv_w), (conv_b_ref, conv_b),
        (conv_rows_ref, conv_rows),
    )
    copies = copies_of(
        small + ((heads_ref, heads_out), (xz_ref.at[0], in_out), (xproj_ref, xproj_out)), sems
    )
    for copy in copies:
        copy.start()
    for copy in copies[: len(small)]:
        copy.wait()
    slots = chosen_ref.shape[1]
    row_id = lax.broadcasted_iota(jnp.int32, (8, slots), 0)
    wanted = jnp.full((8, slots), -1, jnp.int32)
    for r in range(rows):
        away = lax.bitwise_xor(lax.div(source[r], rows), place_ref[0])
        entry = entry_of(away, slots // rows)
        wanted = jnp.where(row_id == r, entry * rows + lax.rem(source[r], rows), wanted)
    chosen = lax.broadcasted_iota(jnp.int32, (8, slots), 1) == wanted
    chosen_ref[...] = jnp.where(chosen, 1.0, 0.0)
    gain_out[...] = gain[...][None]
    taps = conv_rows.shape[0]
    base = conv_b[...]
    for tap in range(taps):
        base = base + conv_w[tap : tap + 1] * conv_rows[tap].astype(F32)
    base_ref[:rows] = base
    base_ref[rows:] = jnp.broadcast_to(conv_w[taps:], base.shape)
    for tap in range(taps - 1):
        new_conv_ref[tap] = conv_rows[tap + 1]
    new_conv_ref[taps - 1] = jnp.zeros_like(conv_rows[0])
    for copy in copies[len(small) :]:
        copy.wait()


def bring(after_ref, xz_ref, gate_out, sems):
    copies = copies_of(((xz_ref.at[1], gate_out),), sems)
    for copy in copies:
        copy.start()
    for copy in copies:
        copy.wait()


def project_in(me_ref, *refs, size):
    arrived_refs = refs[:size]
    (chosen_ref, base_ref, old_conv_ref, gain_ref, heads_w_ref, xproj_ref, in_w_ref, gate_w_ref,
     part_ref, act_ref, gate_ref, new_conv_ref, cols_ref, blocks) = refs[size:]
    rows, cols = cols_ref.shape
    arrived = jnp.concatenate(
        [ref[i].astype(F32) for ref in arrived_refs for i in range(ref.shape[0])], axis=0
    ).astype(BF16)
    routed = jnp.dot(chosen_ref[...].astype(BF16), arrived, preferred_element_type=F32)
    for block in range(blocks.shape[0]):
        blocks[block] = routed[:rows, block * cols : (block + 1) * cols]
    cols_ref[...] = blocks[me_ref[0]]
    scale = lax.rsqrt(jnp.mean(routed * routed, axis=1, keepdims=True) + EPSILON)
    normed = (routed * scale * gain_ref[...]).astype(BF16)
    heads = dot_nt(normed, heads_w_ref[...])[:rows].astype(BF16).astype(F32)
    channel_in = dot_nt(normed, in_w_ref[...])[:rows]
    gate = dot_nt(normed, gate_w_ref[...])[:rows]
    taps = old_conv_ref.shape[0]
    conv_out = base_ref[:rows] + base_ref[rows:] * channel_in
    act = conv_out * sigmoid(conv_out)
    for tap in range(taps - 1):
        new_conv_ref[tap] = old_conv_ref[tap]
    new_conv_ref[taps - 1] = channel_in.astype(BF16)
    act_ref[...] = act
    gate_ref[...] = gate * sigmoid(gate)
    state = dot_nt(act.astype(BF16), xproj_ref[...])
    part_ref[...] = jnp.concatenate([heads, state], axis=1)


def state_step(me_ref, *refs, size, head_width):
    pieces = refs[:size]
    (act_ref, gate_ref, dt_w_ref, dt_b_ref, a_log_ref, ssm_ref, skip_ref, out_w_ref, part_ref,
     new_ssm_ref) = refs[size:]
    state = pieces[0][:, head_width:]
    for piece in pieces[1:]:
        state = state + piece[:, head_width:]
    rows = state.shape[0]
    rank = dt_w_ref.shape[1]
    depth = a_log_ref.shape[0]
    step = dot_nt(state[:, :rank].astype(BF16), dt_w_ref[...]) + dt_b_ref[...]
    step = jnp.maximum(step, 0.0) + jnp.log1p(jnp.exp(-jnp.abs(step)))
    act = act_ref[...]
    rates = jnp.exp(a_log_ref[...])
    maps = jnp.concatenate(
        [state[:, rank:], jnp.zeros((rows, 128 - 2 * depth), F32)], axis=1
    )
    maps = jnp.concatenate([maps, jnp.zeros((8 - rows, 128), F32)], axis=0).T
    outs = []
    for r in range(rows):
        step_row = step[r : r + 1]
        fresh = jnp.exp(-step_row * rates) * ssm_ref[r] + maps[:depth, r : r + 1] * (
            step_row * act[r : r + 1]
        )
        new_ssm_ref[r] = fresh
        outs.append(jnp.sum(maps[depth : 2 * depth, r : r + 1] * fresh, axis=0, keepdims=True))
    state_out = jnp.concatenate(outs, axis=0) + skip_ref[...] * act
    ssm_heads = (state_out * gate_ref[...]).astype(BF16)
    part_ref[...] = jnp.dot(ssm_heads, out_w_ref[...], preferred_element_type=F32).astype(BF16)


def attend(me_ref, lengths_ref, *refs, size, head_width):
    pieces = refs[:size]
    (keys_ref, values_ref, part_ref, new_kv_ref, held) = refs[size:]
    me = me_ref[0]
    stack_pieces(me, pieces, held)
    rows = held.shape[1]
    heads = jnp.concatenate([held[i][:, :head_width] for i in range(size)], axis=1)
    new_kv_ref[...] = heads[:, QUERY_WIDTH:].astype(BF16)

    span = keys_ref.shape[2]
    tall = jnp.concatenate([heads, jnp.zeros((8 - rows, heads.shape[1]), F32)], axis=0)
    row_id = lax.broadcasted_iota(jnp.int32, (8, span), 0)
    slot = lax.broadcasted_iota(jnp.int32, (8, span), 1) + me * span
    length = jnp.zeros((8, span), jnp.int32)
    hole = jnp.zeros((8, span), jnp.int32)
    for r in range(rows):
        count = lengths_ref[r]
        length = jnp.where(row_id == r, count, length)
        hole = jnp.where(
            row_id == r, jnp.where(count >= WINDOW_LENGTH, lax.rem(count, WINDOW_LENGTH), -1), hole
        )
    live = (slot < length) & (slot != hole)
    live = jnp.concatenate([live.astype(F32)] * GROUP, axis=0) > 0.0
    tile_row = lax.rem(lax.broadcasted_iota(jnp.int32, (8 * GROUP, 1), 0), 8)
    own_here = jnp.where(me == 0, 1.0, 0.0)
    numers, tops, totals = [], [], []
    for g in range(KEY_VALUE_HEADS):
        at = QUERY_WIDTH + g * HEAD_SIZE
        new_key = tall[:, at : at + HEAD_SIZE]
        new_value = tall[:, at + KEY_VALUE_WIDTH : at + KEY_VALUE_WIDTH + HEAD_SIZE]
        queries = jnp.concatenate(
            [
                tall[:, j * HEAD_SIZE : (j + 1) * HEAD_SIZE]
                for j in range(g * GROUP, (g + 1) * GROUP)
            ],
            axis=0,
        ) * (HEAD_SIZE ** -0.5)
        own = jnp.sum(queries * jnp.concatenate([new_key] * GROUP, axis=0), axis=1, keepdims=True)
        packed = queries.astype(BF16)
        score = jnp.zeros((8 * GROUP, span), F32)
        for r in range(rows):
            one = jnp.dot(
                packed,
                keys_ref[r, g * HEAD_SIZE : (g + 1) * HEAD_SIZE, :],
                preferred_element_type=F32,
            )
            score = jnp.where(tile_row == r, one, score)
        top = jnp.maximum(
            jnp.max(jnp.where(live, score, -jnp.inf), axis=1, keepdims=True), own
        )
        weight = jnp.where(live, jnp.exp(score - top), 0.0).astype(BF16)
        own_weight = jnp.exp(own - top).astype(BF16).astype(F32) * own_here
        total = jnp.sum(weight.astype(F32), axis=1, keepdims=True) + own_weight
        numer = jnp.zeros((8 * GROUP, HEAD_SIZE), F32)
        for r in range(rows):
            one = dot_nt(weight, values_ref[r, g * HEAD_SIZE : (g + 1) * HEAD_SIZE, :])
            numer = jnp.where(tile_row == r, one, numer)
        numer = numer + own_weight * jnp.concatenate([new_value] * GROUP, axis=0)
        for j in range(GROUP):
            numers.append(numer[8 * j : 8 * j + 8])
            tops.append(top[8 * j : 8 * j + 8])
            totals.append(total[8 * j : 8 * j + 8])
    part_ref[...] = jnp.concatenate(numers + tops + totals, axis=1)[:rows]


def project_out(*refs, size):
    pieces = refs[:size]
    (state_ref, spread_ref, w_ref, y_ref, part_ref) = refs[size:]
    rows = y_ref.shape[0]
    tops = [p[:, QUERY_WIDTH : QUERY_WIDTH + QUERY_HEADS] for p in pieces]
    totals = [p[:, QUERY_WIDTH + QUERY_HEADS :] for p in pieces]
    top = functools.reduce(jnp.maximum, tops)
    factors = [jnp.exp(t - top) for t in tops]
    total = functools.reduce(jnp.add, [f * t for f, t in zip(factors, totals)])
    factors = jnp.concatenate([f / total for f in factors], axis=0)
    high = factors.astype(BF16)
    low = (factors - high.astype(F32)).astype(BF16)
    spread = jnp.dot(high, spread_ref[...], preferred_element_type=F32) + jnp.dot(
        low, spread_ref[...], preferred_element_type=F32
    )
    merged = functools.reduce(
        jnp.add,
        [spread[i * rows : (i + 1) * rows] * p[:, :QUERY_WIDTH] for i, p in enumerate(pieces)],
    )
    y_attn = dot_nt(merged.astype(BF16), w_ref[...])
    y_ref[...] = y_attn
    square = jnp.sum(y_attn * y_attn, axis=1, keepdims=True)
    high = square.astype(BF16)
    rest = square - high.astype(F32)
    low = rest.astype(BF16)
    lowest = (rest - low.astype(F32)).astype(BF16)
    part_ref[...] = jnp.concatenate(
        [state_ref[...], high, low, lowest, jnp.zeros((rows, part_ref.shape[1] - MODEL_WIDTH - 3), BF16)],
        axis=1,
    )


def finish(me_ref, *refs, size):
    pieces = refs[:size]
    y_ref, cols_ref, gain_attn_ref, gain_ssm_ref, out_ref, blocks = refs[size:]
    cols = out_ref.shape[1]
    total = functools.reduce(jnp.add, [p[...].astype(F32) for p in pieces])
    square = jnp.sum(total[:, MODEL_WIDTH : MODEL_WIDTH + 3], axis=1, keepdims=True)
    attn_scale = lax.rsqrt(square / MODEL_WIDTH + EPSILON)
    y_ssm = total[:, :MODEL_WIDTH]
    state_scale = lax.rsqrt(jnp.mean(y_ssm * y_ssm, axis=1, keepdims=True) + EPSILON)
    for block in range(blocks.shape[0]):
        blocks[block] = y_ssm[:, block * cols : (block + 1) * cols]
    mixed = 0.5 * (
        y_ref[...] * attn_scale * gain_attn_ref[...]
        + blocks[me_ref[0]] * state_scale * gain_ssm_ref[...]
    )
    out_ref[...] = (cols_ref[...] + mixed).astype(BF16)


SMEM = pl.BlockSpec(memory_space=pltpu.SMEM)
VMEM = pl.BlockSpec(memory_space=pltpu.VMEM)


def call(body, scalars, blocks, outs, scratch=()):
    return pl.pallas_call(
        body,
        in_specs=[SMEM] * len(scalars) + [VMEM] * len(blocks),
        out_specs=[VMEM] * len(outs),
        out_shape=outs,
        scratch_shapes=scratch,
        compiler_params=pltpu.CompilerParams(vmem_limit_bytes=16 * 1024 * 1024),
    )(*scalars, *blocks)


def shards(
    tokens,
    source,
    lengths,
    cached_key_rows,
    cached_value_rows,
    conv_state,
    ssm_state,
    norm_gain,
    query_key_value_weight,
    w_xz,
    conv_weight,
    conv_bias,
    w_xproj,
    w_dt,
    dt_bias,
    a_log,
    skip_d,
    w_attn_out,
    w_ssm_out,
    gain_attn,
    gain_ssm,
):
    rows = tokens.shape[0]
    narrow = lax.axis_size("narrow")
    me = lax.axis_index("narrow").astype(jnp.int32).reshape(1)
    cols = MODEL_WIDTH // narrow
    head_width = query_key_value_weight.shape[1]
    shape = jax.ShapeDtypeStruct

    place = lax.axis_index("wide").astype(jnp.int32).reshape(1)
    large = (query_key_value_weight.T, w_xproj.T, w_xz.transpose(1, 2, 0))
    small = (source, norm_gain, conv_weight, conv_bias[None], conv_state.transpose(1, 0, 2))
    slots = rows * lax.axis_size("wide")
    half = large[2].shape[1:]
    pinned = [pltpu.with_memory_space_constraint(a, pltpu.HBM) for a in small + large]
    anywhere = pl.BlockSpec(memory_space=pl.ANY)
    prepared = pl.pallas_call(
        prepare,
        in_specs=[SMEM] + [anywhere] * len(pinned),
        out_specs=[VMEM] * 7,
        out_shape=[
            pltpu.VMEM((8, slots), F32),
            pltpu.VMEM((2 * rows, cols), F32),
            pltpu.VMEM(small[4].shape, BF16),
            pltpu.VMEM((1, MODEL_WIDTH), F32),
            pltpu.VMEM(large[0].shape, BF16),
            pltpu.VMEM(large[1].shape, BF16),
            pltpu.VMEM(half, BF16),
        ],
        scratch_shapes=[pltpu.SMEM(source.shape, jnp.int32)]
        + [pltpu.VMEM(a.shape, a.dtype) for a in small[1:]]
        + [pltpu.SemaphoreType.DMA((6 + 2 * (PARTS + 1),))],
        compiler_params=pltpu.CompilerParams(vmem_limit_bytes=4 * 1024 * 1024),
    )(place, *pinned)
    arrived = gather_xor(tokens, "wide", prepared[:1])
    (gate_w,) = pl.pallas_call(
        bring,
        in_specs=[anywhere] * 2,
        out_specs=[VMEM],
        out_shape=[pltpu.VMEM(half, BF16)],
        scratch_shapes=[pltpu.SemaphoreType.DMA((PARTS + 1,))],
        compiler_params=pltpu.CompilerParams(vmem_limit_bytes=4 * 1024 * 1024),
    )(arrived[0], pinned[-1])
    part_width = head_width + w_xproj.shape[1]
    part, act, gate, new_conv, routed_cols = call(
        functools.partial(project_in, size=len(arrived)),
        (me,),
        (*arrived, *prepared, gate_w),
        (
            shape((rows, part_width), F32),
            shape((rows, cols), F32),
            shape((rows, cols), F32),
            shape((conv_state.shape[1], rows, cols), BF16),
            shape((rows, cols), F32),
        ),
        (pltpu.VMEM((narrow, rows, cols), F32),),
    )
    pieces = exchange(part, "narrow")
    second, new_kv = call(
        functools.partial(attend, size=narrow, head_width=head_width),
        (me, lengths),
        (*pieces, cached_key_rows.transpose(0, 2, 1), cached_value_rows.transpose(0, 2, 1)),
        (
            shape((rows, QUERY_WIDTH + 2 * QUERY_HEADS), F32),
            shape((rows, 2 * KEY_VALUE_WIDTH), BF16),
        ),
        (pltpu.VMEM((narrow, rows, part_width), F32),),
    )
    state_part, new_ssm = call(
        functools.partial(state_step, size=narrow, head_width=head_width),
        (me,),
        (
            *pieces, act, gate, w_dt.T, dt_bias[None], a_log, ssm_state, skip_d[None], w_ssm_out,
        ),
        (shape((rows, MODEL_WIDTH), BF16), shape(ssm_state.shape, F32)),
    )
    pieces = exchange(second, "narrow")
    spread = (
        lax.broadcasted_iota(jnp.int32, (QUERY_HEADS, QUERY_WIDTH), 1) // HEAD_SIZE
        == lax.broadcasted_iota(jnp.int32, (QUERY_HEADS, QUERY_WIDTH), 0)
    ).astype(BF16)
    y_attn, third = call(
        functools.partial(project_out, size=narrow),
        (),
        (*pieces, state_part, spread, w_attn_out.T),
        (shape((rows, cols), F32), shape((rows, MODEL_WIDTH + 64), BF16)),
    )
    pieces = exchange(third, "narrow")
    (out,) = call(
        functools.partial(finish, size=narrow),
        (me,),
        (*pieces, y_attn, routed_cols, gain_attn[None], gain_ssm[None]),
        (shape((rows, cols), BF16),),
        (pltpu.VMEM((narrow, rows, cols), F32),),
    )
    return (out, new_kv, new_conv.transpose(1, 0, 2), new_ssm)


def solution(mesh):
    placed = (
        P("wide", None),
        P("wide"),
        P("wide"),
        P("wide", "narrow", None),
        P("wide", "narrow", None),
        P("wide", None, "narrow"),
        P("wide", None, "narrow"),
        P(),
        P(None, "narrow"),
        P(None, None, "narrow"),
        P(None, "narrow"),
        P("narrow"),
        P("narrow", None),
        P(None, "narrow"),
        P("narrow"),
        P(None, "narrow"),
        P("narrow"),
        P(None, "narrow"),
        P("narrow", None),
        P("narrow"),
        P("narrow"),
    )
    return jax.shard_map(
        shards,
        mesh=mesh,
        in_specs=placed,
        out_specs=(
            P("wide", "narrow"),
            P("wide", None),
            P("wide", None, "narrow"),
            P("wide", None, "narrow"),
        ),
        check_vma=False,
    )
```

```python
import functools
import jax
import jax.numpy as jnp
from jax import lax
from jax.experimental import pallas as pl
from jax.experimental.pallas import tpu as pltpu
from jax.sharding import PartitionSpec as P

MODEL_WIDTH = 1600
QUERY_HEADS = 25
KEY_VALUE_HEADS = 5
HEAD_SIZE = 64
WINDOW_LENGTH = 1024
GROUP = QUERY_HEADS // KEY_VALUE_HEADS
QUERY_WIDTH = QUERY_HEADS * HEAD_SIZE
KEY_VALUE_WIDTH = KEY_VALUE_HEADS * HEAD_SIZE


EPSILON = 1e-06
PARTS = 4

NT = (((1,), (1,)), ((), ()))
F32 = jnp.float32
BF16 = jnp.bfloat16


def dot_nt(a, b):
    return lax.dot_general(a, b, NT, preferred_element_type=F32)


def sigmoid(v):
    return 1.0 / (1.0 + jnp.exp(-v))


def exchange(part, axis):
    size = lax.axis_size(axis)
    return [part] + [
        lax.ppermute(part, axis, [(i, (i + step) % size) for i in range(size)])
        for step in range(1, size)
    ]


def join(*refs):
    *given, out_ref = refs
    at = 0
    for ref in given:
        out_ref[at : at + ref.shape[0]] = ref[...]
        at += ref.shape[0]


def digits_of(size):
    assert size & (size - 1) == 0
    rounds, done, total = [], 0, size.bit_length() - 1
    while done < total:
        count = 1 if (total - done) % 2 else 2
        rounds.append((done, count))
        done += count
    return rounds


def gather_xor(part, axis, beside):
    size = lax.axis_size(axis)
    blocks = [part[None]]
    for place, count in digits_of(size):
        held = blocks[0]
        if len(blocks) > 1:
            entries = sum(b.shape[0] for b in blocks)
            (held,) = call(
                join, (), blocks, (jax.ShapeDtypeStruct((entries, *part.shape), part.dtype),), after=beside
            )
            beside = ()
        blocks = [held] + [
            lax.ppermute(held, axis, [(i, i ^ (step << place)) for i in range(size)])
            for step in range((1 << count) - 1, 0, -1)
        ]
    return blocks


def entry_of(away, size):
    entry, done = jnp.int32(0), 0
    for place, count in digits_of(size):
        top = (1 << count) - 1
        digit = lax.bitwise_and(lax.shift_right_logical(away, place), top)
        entry = entry + lax.shift_left(lax.bitwise_and(top + 1 - digit, top), done)
        done += count
    return entry


def stack_pieces(me, pieces, held):
    size = len(pieces)
    for step, piece in enumerate(pieces):
        held[lax.rem(me - step + size, size)] = piece[...]


def cut(rows, count):
    step = -(-rows // (16 * count)) * 16
    return [(at, min(step, rows - at)) for at in range(0, rows, step)]


def copies_of(pairs, sems):
    copies = []
    for origin, to in pairs:
        if len(to.shape) == 2 and to.shape[0] >= 256:
            ranges = [pl.ds(at, size) for at, size in cut(to.shape[0], PARTS)]
            copies += [(origin.at[r], to.at[r]) for r in ranges]
        else:
            copies.append((origin, to))
    return [pltpu.make_async_copy(origin, to, sems.at[i]) for i, (origin, to) in enumerate(copies)]


def prepare(
    place_ref, source_ref, gain_ref, conv_w_ref, conv_b_ref, conv_rows_ref, heads_ref, xproj_ref, xz_ref,
    chosen_ref, base_ref, new_conv_ref, gain_out, heads_out, xproj_out, in_out,
    source, gain, conv_w, conv_b, conv_rows, sems,
):
    rows = source.shape[0]
    small = (
        (source_ref, source), (gain_ref, gain), (conv_w_ref, conv_w), (conv_b_ref, conv_b),
        (conv_rows_ref, conv_rows),
    )
    copies = copies_of(
        small + ((heads_ref, heads_out), (xz_ref.at[0], in_out), (xproj_ref, xproj_out)), sems
    )
    for copy in copies:
        copy.start()
    for copy in copies[: len(small)]:
        copy.wait()
    slots = chosen_ref.shape[1]
    row_id = lax.broadcasted_iota(jnp.int32, (8, slots), 0)
    wanted = jnp.full((8, slots), -1, jnp.int32)
    for r in range(rows):
        away = lax.bitwise_xor(lax.div(source[r], rows), place_ref[0])
        entry = entry_of(away, slots // rows)
        wanted = jnp.where(row_id == r, entry * rows + lax.rem(source[r], rows), wanted)
    chosen = lax.broadcasted_iota(jnp.int32, (8, slots), 1) == wanted
    chosen_ref[...] = jnp.where(chosen, 1.0, 0.0)
    gain_out[...] = gain[...][None]
    taps = conv_rows.shape[0]
    base = conv_b[...]
    for tap in range(taps):
        base = base + conv_w[tap : tap + 1] * conv_rows[tap].astype(F32)
    base_ref[:rows] = base
    base_ref[rows:] = jnp.broadcast_to(conv_w[taps:], base.shape)
    for tap in range(taps - 1):
        new_conv_ref[tap] = conv_rows[tap + 1]
    new_conv_ref[taps - 1] = jnp.zeros_like(conv_rows[0])
    for copy in copies[len(small) :]:
        copy.wait()


def bring(after_ref, xz_ref, gate_out, sems):
    copies = copies_of(((xz_ref.at[1], gate_out),), sems)
    for copy in copies:
        copy.start()
    for copy in copies:
        copy.wait()


def project_in(me_ref, *refs, size):
    arrived_refs = refs[:size]
    (chosen_ref, base_ref, old_conv_ref, gain_ref, heads_w_ref, xproj_ref, in_w_ref, part_ref,
     act_ref, normed_ref, new_conv_ref, cols_ref, blocks) = refs[size:]
    rows, cols = cols_ref.shape
    arrived = jnp.concatenate(
        [ref[i].astype(F32) for ref in arrived_refs for i in range(ref.shape[0])], axis=0
    ).astype(BF16)
    routed = jnp.dot(chosen_ref[...].astype(BF16), arrived, preferred_element_type=F32)
    for block in range(blocks.shape[0]):
        blocks[block] = routed[:rows, block * cols : (block + 1) * cols]
    cols_ref[...] = blocks[me_ref[0]]
    scale = lax.rsqrt(jnp.mean(routed * routed, axis=1, keepdims=True) + EPSILON)
    normed = (routed * scale * gain_ref[...]).astype(BF16)
    normed_ref[...] = normed
    channel_in = dot_nt(normed, in_w_ref[...])[:rows]
    heads = dot_nt(normed, heads_w_ref[...])[:rows].astype(BF16).astype(F32)
    taps = old_conv_ref.shape[0]
    conv_out = base_ref[:rows] + base_ref[rows:] * channel_in
    act = conv_out * sigmoid(conv_out)
    for tap in range(taps - 1):
        new_conv_ref[tap] = old_conv_ref[tap]
    new_conv_ref[taps - 1] = channel_in.astype(BF16)
    act_ref[...] = act
    state = dot_nt(act.astype(BF16), xproj_ref[...])
    part_ref[...] = jnp.concatenate([heads, state], axis=1)


def project_gate(normed_ref, gate_w_ref, gate_ref):
    gate = dot_nt(normed_ref[...], gate_w_ref[...])[: gate_ref.shape[0]]
    gate_ref[...] = gate * sigmoid(gate)


def state_step(me_ref, *refs, size, head_width):
    pieces = refs[:size]
    (act_ref, gate_ref, dt_w_ref, dt_b_ref, a_log_ref, ssm_ref, skip_ref, out_w_ref, part_ref,
     new_ssm_ref) = refs[size:]
    state = pieces[0][:, head_width:]
    for piece in pieces[1:]:
        state = state + piece[:, head_width:]
    rows = state.shape[0]
    rank = dt_w_ref.shape[1]
    depth = a_log_ref.shape[0]
    step = dot_nt(state[:, :rank].astype(BF16), dt_w_ref[...]) + dt_b_ref[...]
    step = jnp.maximum(step, 0.0) + jnp.log1p(jnp.exp(-jnp.abs(step)))
    act = act_ref[...]
    rates = jnp.exp(a_log_ref[...])
    maps = jnp.concatenate(
        [state[:, rank:], jnp.zeros((rows, 128 - 2 * depth), F32)], axis=1
    )
    maps = jnp.concatenate([maps, jnp.zeros((8 - rows, 128), F32)], axis=0).T
    outs = []
    for r in range(rows):
        step_row = step[r : r + 1]
        fresh = jnp.exp(-step_row * rates) * ssm_ref[r] + maps[:depth, r : r + 1] * (
            step_row * act[r : r + 1]
        )
        new_ssm_ref[r] = fresh
        outs.append(jnp.sum(maps[depth : 2 * depth, r : r + 1] * fresh, axis=0, keepdims=True))
    state_out = jnp.concatenate(outs, axis=0) + skip_ref[...] * act
    ssm_heads = (state_out * gate_ref[...]).astype(BF16)
    part_ref[...] = jnp.dot(ssm_heads, out_w_ref[...], preferred_element_type=F32).astype(BF16)


def attend(me_ref, lengths_ref, *refs, size, head_width):
    pieces = refs[:size]
    (keys_ref, values_ref, part_ref, new_kv_ref, held) = refs[size:]
    me = me_ref[0]
    stack_pieces(me, pieces, held)
    rows = held.shape[1]
    heads = jnp.concatenate([held[i][:, :head_width] for i in range(size)], axis=1)
    new_kv_ref[...] = heads[:, QUERY_WIDTH:].astype(BF16)
    tall = jnp.concatenate([heads, jnp.zeros((8 - rows, heads.shape[1]), F32)], axis=0)
    tall = jnp.concatenate([tall, jnp.zeros((8, -tall.shape[1] % 128), F32)], axis=1)
    lane = lax.broadcasted_iota(jnp.int32, (8, 128), 1)
    row = lax.broadcasted_iota(jnp.int32, (8, 128), 0)
    first = lane < HEAD_SIZE

    turned = {}

    def twice(at):
        tile = at // 128
        if tile not in turned:
            line = tall[:, tile * 128 : tile * 128 + 128]
            turned[tile] = (line, pltpu.roll(line, HEAD_SIZE, 1))
        line, other = turned[tile]
        return jnp.where(first, line, other) if at % 128 == 0 else jnp.where(first, other, line)

    blocks = -(-rows // 2)
    own_block = [
        jnp.where(row == jnp.where(first, 2 * i, 2 * i + 1), 1.0, 0.0) for i in range(blocks)
    ]
    half = jnp.where(first, HEAD_SIZE ** -0.5, 0.0)
    groups = range(KEY_VALUE_HEADS)
    queries = [[twice(j * HEAD_SIZE) for j in range(g * GROUP, (g + 1) * GROUP)] for g in groups]
    scores = []
    for g in groups:
        spread = jnp.concatenate(
            [
                jnp.concatenate([q * (HEAD_SIZE ** -0.5) * mask for mask in own_block], axis=1)
                for q in queries[g]
            ],
            axis=0,
        ).astype(BF16)
        keys = jnp.concatenate(
            [keys_ref[r, g * HEAD_SIZE : (g + 1) * HEAD_SIZE, :] for r in range(rows)], axis=0
        )
        scores.append(jnp.dot(spread, keys, preferred_element_type=F32))
    new_keys = [twice(QUERY_WIDTH + g * HEAD_SIZE) * half for g in groups]
    own = [
        jnp.sum(
            jnp.concatenate([q * new_keys[g] for q in queries[g]], axis=0), axis=1, keepdims=True
        )
        for g in groups
    ]

    span = keys_ref.shape[2]
    row_id = lax.broadcasted_iota(jnp.int32, (8, span), 0)
    slot = lax.broadcasted_iota(jnp.int32, (8, span), 1) + me * span
    length = jnp.zeros((8, span), jnp.int32)
    hole = jnp.zeros((8, span), jnp.int32)
    for r in range(rows):
        count = lengths_ref[r]
        length = jnp.where(row_id == r, count, length)
        hole = jnp.where(
            row_id == r, jnp.where(count >= WINDOW_LENGTH, lax.rem(count, WINDOW_LENGTH), -1), hole
        )
    live = jnp.where((slot < length) & (slot != hole), 1.0, 0.0)
    live = jnp.concatenate([live] * GROUP, axis=0) > 0.0
    tops = [
        jnp.maximum(
            jnp.max(jnp.where(live, scores[g], -jnp.inf), axis=1, keepdims=True), own[g]
        )
        for g in groups
    ]
    weights = [
        jnp.where(live, jnp.exp(scores[g] - tops[g]), 0.0).astype(BF16) for g in groups
    ]
    own_here = jnp.where(me == 0, 1.0, 0.0)
    own_weights = [
        jnp.exp(own[g] - tops[g]).astype(BF16).astype(F32) * own_here for g in groups
    ]
    products = []
    for g in groups:
        values = jnp.concatenate(
            [values_ref[r, g * HEAD_SIZE : (g + 1) * HEAD_SIZE, :] for r in range(rows)], axis=0
        )
        products.append(dot_nt(weights[g], values))
    totals = [
        jnp.sum(weights[g].astype(F32), axis=1, keepdims=True) + own_weights[g] for g in groups
    ]
    stats = jnp.zeros((8, 128), F32)
    numers = []
    for g in groups:
        new_value = twice(QUERY_WIDTH + KEY_VALUE_WIDTH + g * HEAD_SIZE)
        for k in range(GROUP):
            j = g * GROUP + k
            at = slice(8 * k, 8 * k + 8)
            folded = products[g][at, :128] * own_block[0]
            for i in range(1, blocks):
                folded = folded + products[g][at, 128 * i : 128 * i + 128] * own_block[i]
            numers.append(
                folded + pltpu.roll(folded, HEAD_SIZE, 1) + own_weights[g][at] * new_value
            )
            stats = jnp.where(lane == j, tops[g][at], stats)
            stats = jnp.where(lane == QUERY_HEADS + j, totals[g][at], stats)
    lines = [
        jnp.where(first, numers[j], numers[j + 1]) for j in range(0, QUERY_HEADS - 1, 2)
    ]
    high = stats.astype(BF16).astype(F32)
    middle = (stats - high).astype(BF16).astype(F32)
    low = stats - high - middle
    lines.append(jnp.where(first, numers[-1], pltpu.roll(high, HEAD_SIZE, 1)))
    lines.append(jnp.where(first, middle, pltpu.roll(low, HEAD_SIZE, 1)))
    part_ref[...] = jnp.concatenate(lines, axis=1)[:rows].astype(BF16)


def project_out(*refs, size):
    pieces = refs[:size]
    (state_ref, spread_ref, w_ref, y_ref, part_ref) = refs[size:]
    rows = y_ref.shape[0]
    stats = [
        functools.reduce(
            jnp.add,
            [
                p[:, QUERY_WIDTH + i * HEAD_SIZE : QUERY_WIDTH + (i + 1) * HEAD_SIZE].astype(F32)
                for i in range(3)
            ],
        )
        for p in pieces
    ]
    tops = [t[:, :QUERY_HEADS] for t in stats]
    totals = [t[:, QUERY_HEADS : 2 * QUERY_HEADS] for t in stats]
    top = functools.reduce(jnp.maximum, tops)
    factors = [jnp.exp(t - top) for t in tops]
    total = functools.reduce(jnp.add, [f * t for f, t in zip(factors, totals)])
    factors = jnp.concatenate([f / total for f in factors], axis=0)
    high = factors.astype(BF16)
    low = (factors - high.astype(F32)).astype(BF16)
    spread = jnp.dot(high, spread_ref[...], preferred_element_type=F32) + jnp.dot(
        low, spread_ref[...], preferred_element_type=F32
    )
    merged = functools.reduce(
        jnp.add,
        [spread[i * rows : (i + 1) * rows] * p[:, :QUERY_WIDTH].astype(F32) for i, p in enumerate(pieces)],
    )
    y_attn = dot_nt(merged.astype(BF16), w_ref[...])
    y_ref[...] = y_attn
    square = jnp.sum(y_attn * y_attn, axis=1, keepdims=True)
    high = square.astype(BF16)
    rest = square - high.astype(F32)
    low = rest.astype(BF16)
    lowest = (rest - low.astype(F32)).astype(BF16)
    part_ref[...] = jnp.concatenate(
        [state_ref[...], high, low, lowest, jnp.zeros((rows, part_ref.shape[1] - MODEL_WIDTH - 3), BF16)],
        axis=1,
    )


def finish(me_ref, *refs, size):
    pieces = refs[:size]
    y_ref, cols_ref, gain_attn_ref, gain_ssm_ref, out_ref, blocks = refs[size:]
    cols = out_ref.shape[1]
    total = functools.reduce(jnp.add, [p[...].astype(F32) for p in pieces])
    square = jnp.sum(total[:, MODEL_WIDTH : MODEL_WIDTH + 3], axis=1, keepdims=True)
    attn_scale = lax.rsqrt(square / MODEL_WIDTH + EPSILON)
    y_ssm = total[:, :MODEL_WIDTH]
    state_scale = lax.rsqrt(jnp.mean(y_ssm * y_ssm, axis=1, keepdims=True) + EPSILON)
    for block in range(blocks.shape[0]):
        blocks[block] = y_ssm[:, block * cols : (block + 1) * cols]
    mixed = 0.5 * (
        y_ref[...] * attn_scale * gain_attn_ref[...]
        + blocks[me_ref[0]] * state_scale * gain_ssm_ref[...]
    )
    out_ref[...] = (cols_ref[...] + mixed).astype(BF16)


SMEM = pl.BlockSpec(memory_space=pltpu.SMEM)
VMEM = pl.BlockSpec(memory_space=pltpu.VMEM)


def call(body, scalars, blocks, outs, scratch=(), after=()):
    def run(*refs):
        body(*refs[len(after) :])

    return pl.pallas_call(
        run,
        in_specs=[pl.BlockSpec(memory_space=pl.ANY)] * len(after)
        + [SMEM] * len(scalars)
        + [VMEM] * len(blocks),
        out_specs=[VMEM] * len(outs),
        out_shape=outs,
        scratch_shapes=scratch,
        compiler_params=pltpu.CompilerParams(vmem_limit_bytes=16 * 1024 * 1024),
    )(*after, *scalars, *blocks)


def shards(
    tokens,
    source,
    lengths,
    cached_key_rows,
    cached_value_rows,
    conv_state,
    ssm_state,
    norm_gain,
    query_key_value_weight,
    w_xz,
    conv_weight,
    conv_bias,
    w_xproj,
    w_dt,
    dt_bias,
    a_log,
    skip_d,
    w_attn_out,
    w_ssm_out,
    gain_attn,
    gain_ssm,
):
    rows = tokens.shape[0]
    narrow = lax.axis_size("narrow")
    me = lax.axis_index("narrow").astype(jnp.int32).reshape(1)
    cols = MODEL_WIDTH // narrow
    head_width = query_key_value_weight.shape[1]
    shape = jax.ShapeDtypeStruct

    place = lax.axis_index("wide").astype(jnp.int32).reshape(1)
    large = (query_key_value_weight.T, w_xproj.T, w_xz.transpose(1, 2, 0))
    small = (source, norm_gain, conv_weight, conv_bias[None], conv_state.transpose(1, 0, 2))
    slots = rows * lax.axis_size("wide")
    half = large[2].shape[1:]
    pinned = [pltpu.with_memory_space_constraint(a, pltpu.HBM) for a in small + large]
    anywhere = pl.BlockSpec(memory_space=pl.ANY)
    prepared = pl.pallas_call(
        prepare,
        in_specs=[SMEM] + [anywhere] * len(pinned),
        out_specs=[VMEM] * 7,
        out_shape=[
            pltpu.VMEM((8, slots), F32),
            pltpu.VMEM((2 * rows, cols), F32),
            pltpu.VMEM(small[4].shape, BF16),
            pltpu.VMEM((1, MODEL_WIDTH), F32),
            pltpu.VMEM(large[0].shape, BF16),
            pltpu.VMEM(large[1].shape, BF16),
            pltpu.VMEM(half, BF16),
        ],
        scratch_shapes=[pltpu.SMEM(source.shape, jnp.int32)]
        + [pltpu.VMEM(a.shape, a.dtype) for a in small[1:]]
        + [pltpu.SemaphoreType.DMA((6 + 2 * (PARTS + 1),))],
        compiler_params=pltpu.CompilerParams(vmem_limit_bytes=4 * 1024 * 1024),
    )(place, *pinned)
    arrived = gather_xor(tokens, "wide", prepared[:1])
    (gate_w,) = pl.pallas_call(
        bring,
        in_specs=[anywhere] * 2,
        out_specs=[VMEM],
        out_shape=[pltpu.VMEM(half, BF16)],
        scratch_shapes=[pltpu.SemaphoreType.DMA((PARTS + 1,))],
        compiler_params=pltpu.CompilerParams(vmem_limit_bytes=4 * 1024 * 1024),
    )(arrived[0], pinned[-1])
    part_width = head_width + w_xproj.shape[1]
    part, act, normed, new_conv, routed_cols = call(
        functools.partial(project_in, size=len(arrived)),
        (me,),
        (*arrived, *prepared),
        (
            shape((rows, part_width), F32),
            shape((rows, cols), F32),
            shape((8, MODEL_WIDTH), BF16),
            shape((conv_state.shape[1], rows, cols), BF16),
            shape((rows, cols), F32),
        ),
        (pltpu.VMEM((narrow, rows, cols), F32),),
        after=(gate_w,),
    )
    pieces = exchange(part, "narrow")
    (gate,) = call(project_gate, (), (normed, gate_w), (shape((rows, cols), F32),))
    second, new_kv = call(
        functools.partial(attend, size=narrow, head_width=head_width),
        (me, lengths),
        (*pieces, cached_key_rows.transpose(0, 2, 1), cached_value_rows.transpose(0, 2, 1)),
        (
            shape((rows, QUERY_WIDTH + 3 * HEAD_SIZE), BF16),
            shape((rows, 2 * KEY_VALUE_WIDTH), BF16),
        ),
        (pltpu.VMEM((narrow, rows, part_width), F32),),
        after=(gate,),
    )
    state_part, new_ssm = call(
        functools.partial(state_step, size=narrow, head_width=head_width),
        (me,),
        (
            *pieces, act, gate, w_dt.T, dt_bias[None], a_log, ssm_state, skip_d[None], w_ssm_out,
        ),
        (shape((rows, MODEL_WIDTH), BF16), shape(ssm_state.shape, F32)),
    )
    pieces = exchange(second, "narrow")
    spread = (
        lax.broadcasted_iota(jnp.int32, (QUERY_HEADS, QUERY_WIDTH), 1) // HEAD_SIZE
        == lax.broadcasted_iota(jnp.int32, (QUERY_HEADS, QUERY_WIDTH), 0)
    ).astype(BF16)
    y_attn, third = call(
        functools.partial(project_out, size=narrow),
        (),
        (*pieces, state_part, spread, w_attn_out.T),
        (shape((rows, cols), F32), shape((rows, MODEL_WIDTH + 64), BF16)),
    )
    pieces = exchange(third, "narrow")
    (out,) = call(
        functools.partial(finish, size=narrow),
        (me,),
        (*pieces, y_attn, routed_cols, gain_attn[None], gain_ssm[None]),
        (shape((rows, cols), BF16),),
        (pltpu.VMEM((narrow, rows, cols), F32),),
    )
    return (out, new_kv, new_conv.transpose(1, 0, 2), new_ssm)


def solution(mesh):
    placed = (
        P("wide", None),
        P("wide"),
        P("wide"),
        P("wide", "narrow", None),
        P("wide", "narrow", None),
        P("wide", None, "narrow"),
        P("wide", None, "narrow"),
        P(),
        P(None, "narrow"),
        P(None, None, "narrow"),
        P(None, "narrow"),
        P("narrow"),
        P("narrow", None),
        P(None, "narrow"),
        P("narrow"),
        P(None, "narrow"),
        P("narrow"),
        P(None, "narrow"),
        P("narrow", None),
        P("narrow"),
        P("narrow"),
    )
    return jax.shard_map(
        shards,
        mesh=mesh,
        in_specs=placed,
        out_specs=(
            P("wide", "narrow"),
            P("wide", None),
            P("wide", None, "narrow"),
            P("wide", None, "narrow"),
        ),
        check_vma=False,
    )
```

```python
import functools
import jax
import jax.numpy as jnp
from jax import lax
from jax.experimental import pallas as pl
from jax.experimental.pallas import tpu as pltpu
from jax.sharding import PartitionSpec as P

MODEL_WIDTH = 1600
QUERY_HEADS = 25
KEY_VALUE_HEADS = 5
HEAD_SIZE = 64
WINDOW_LENGTH = 1024
GROUP = QUERY_HEADS // KEY_VALUE_HEADS
QUERY_WIDTH = QUERY_HEADS * HEAD_SIZE
KEY_VALUE_WIDTH = KEY_VALUE_HEADS * HEAD_SIZE


EPSILON = 1e-06
PARTS = 4

NT = (((1,), (1,)), ((), ()))
F32 = jnp.float32
BF16 = jnp.bfloat16


def dot_nt(a, b):
    return lax.dot_general(a, b, NT, preferred_element_type=F32)


def sigmoid(v):
    return 1.0 / (1.0 + jnp.exp(-v))


def exchange(part, axis):
    size = lax.axis_size(axis)
    return [part] + [
        lax.ppermute(part, axis, [(i, (i + step) % size) for i in range(size)])
        for step in range(1, size)
    ]


def join(*refs):
    *given, out_ref = refs
    at = 0
    for ref in given:
        out_ref[at : at + ref.shape[0]] = ref[...]
        at += ref.shape[0]


def digits_of(size):
    assert size & (size - 1) == 0
    rounds, done, total = [], 0, size.bit_length() - 1
    while done < total:
        count = 1 if (total - done) % 2 else 2
        rounds.append((done, count))
        done += count
    return rounds


def gather_xor(part, axis, core_axis, beside):
    size, cores = lax.axis_size(axis), lax.axis_size(core_axis)
    blocks = [part[None]]
    rounds = digits_of(size)
    for place, count in rounds:
        held = blocks[0]
        if len(blocks) > 1:
            entries = sum(b.shape[0] for b in blocks)
            (held,) = call(
                join, (), blocks, (jax.ShapeDtypeStruct((entries, *part.shape), part.dtype),), after=beside
            )
            beside = ()
        if count == 2 and place == rounds[-1][0]:

            def fetch(even, odd):
                moves = [
                    (i * cores + c, (i ^ (step << place)) * cores + c)
                    for i in range(size)
                    for c in range(cores)
                    for step in [odd if c % 2 else even]
                    if step
                ]
                return lax.ppermute(held, (axis, core_axis), moves)

            far, near = fetch(3, 2), fetch(0, 1)
            near_swap = lax.ppermute(near, core_axis, [(c, c - 1) for c in range(1, cores, 2)])
            far_swap = lax.ppermute(far, core_axis, [(c, c ^ 1) for c in range(cores)])
            blocks = [held, near, near_swap, far, far_swap]
        else:
            blocks = [held] + [
                lax.ppermute(held, axis, [(i, i ^ (step << place)) for i in range(size)])
                for step in range((1 << count) - 1, 0, -1)
            ]
    return blocks


def entries_of(size):
    rounds = digits_of(size)
    return (5 * size) // 4 if rounds[-1][1] == 2 else size


def entry_of(away, size, core):
    entry, done = jnp.int32(0), 0
    rounds = digits_of(size)
    for place, count in rounds:
        top = (1 << count) - 1
        digit = lax.bitwise_and(lax.shift_right_logical(away, place), top)
        if count == 2 and place == rounds[-1][0]:
            odd = lax.bitwise_and(core, 1)
            near = 2 - odd
            far = jnp.where(digit == 3 - odd, 3, 4)
            block = jnp.where(digit == 0, 0, jnp.where(digit == 1, near, far))
        else:
            block = lax.bitwise_and(top + 1 - digit, top)
        entry = entry + block * (1 << done)
        done += count
    return entry


def stack_pieces(me, pieces, held):
    size = len(pieces)
    for step, piece in enumerate(pieces):
        held[lax.rem(me - step + size, size)] = piece[...]


def cut(rows, count):
    step = -(-rows // (16 * count)) * 16
    return [(at, min(step, rows - at)) for at in range(0, rows, step)]


def copies_of(pairs, sems):
    copies = []
    for origin, to in pairs:
        if len(to.shape) == 2 and to.shape[0] >= 256:
            ranges = [pl.ds(at, size) for at, size in cut(to.shape[0], PARTS)]
            copies += [(origin.at[r], to.at[r]) for r in ranges]
        else:
            copies.append((origin, to))
    return [pltpu.make_async_copy(origin, to, sems.at[i]) for i, (origin, to) in enumerate(copies)]


def live_slots(lengths, span, me):
    row_id = lax.broadcasted_iota(jnp.int32, (8, span), 0)
    slot = lax.broadcasted_iota(jnp.int32, (8, span), 1) + me * span
    length = jnp.zeros((8, span), jnp.int32)
    hole = jnp.zeros((8, span), jnp.int32)
    for r in range(lengths.shape[0]):
        count = lengths[r]
        length = jnp.where(row_id == r, count, length)
        hole = jnp.where(
            row_id == r, jnp.where(count >= WINDOW_LENGTH, lax.rem(count, WINDOW_LENGTH), -1), hole
        )
    return jnp.where((slot < length) & (slot != hole), 1.0, 0.0)


def prepare(
    source_ref, lengths_ref, gain_ref, conv_w_ref, conv_b_ref, conv_rows_ref, heads_ref, xproj_ref, xz_ref,
    chosen_ref, live_ref, base_ref, new_conv_ref, gain_out, heads_out, xproj_out, in_out,
    source, lengths, gain, conv_w, conv_b, conv_rows, sems, *, size,
):
    rows = source.shape[0]
    small = (
        (source_ref, source), (lengths_ref, lengths), (gain_ref, gain), (conv_w_ref, conv_w), (conv_b_ref, conv_b),
        (conv_rows_ref, conv_rows),
    )
    copies = copies_of(
        small + ((heads_ref, heads_out), (xz_ref.at[0], in_out), (xproj_ref, xproj_out)), sems
    )
    for copy in copies:
        copy.start()
    for copy in copies[: len(small)]:
        copy.wait()
    me = lax.axis_index("narrow")
    slots = chosen_ref.shape[1]
    row_id = lax.broadcasted_iota(jnp.int32, (8, slots), 0)
    wanted = jnp.full((8, slots), -1, jnp.int32)
    for r in range(rows):
        away = lax.bitwise_xor(lax.div(source[r], rows), lax.axis_index("wide"))
        entry = entry_of(away, size, me)
        wanted = jnp.where(row_id == r, entry * rows + lax.rem(source[r], rows), wanted)
    chosen = lax.broadcasted_iota(jnp.int32, (8, slots), 1) == wanted
    chosen_ref[...] = jnp.where(chosen, 1.0, 0.0)
    live_ref[...] = live_slots(lengths, live_ref.shape[1], me)
    gain_out[...] = gain[...][None]
    taps = conv_rows.shape[0]
    base = conv_b[...]
    for tap in range(taps):
        base = base + conv_w[tap : tap + 1] * conv_rows[tap].astype(F32)
    base_ref[:rows] = base
    base_ref[rows:] = jnp.broadcast_to(conv_w[taps:], base.shape)
    for tap in range(taps - 1):
        new_conv_ref[tap] = conv_rows[tap + 1]
    new_conv_ref[taps - 1] = jnp.zeros_like(conv_rows[0])
    for copy in copies[len(small) :]:
        copy.wait()


def project_in(*refs, size):
    arrived_refs = refs[:size]
    (chosen_ref, base_ref, gain_ref, heads_w_ref, xproj_ref, in_w_ref, part_ref, act_ref,
     normed_ref, channel_ref, cols_ref, blocks) = refs[size:]
    rows, cols = cols_ref.shape
    arrived = jnp.concatenate(
        [ref[i].astype(F32) for ref in arrived_refs for i in range(ref.shape[0])], axis=0
    ).astype(BF16)
    routed = jnp.dot(chosen_ref[...].astype(BF16), arrived, preferred_element_type=F32)
    for block in range(blocks.shape[0]):
        blocks[block] = routed[:rows, block * cols : (block + 1) * cols]
    cols_ref[...] = blocks[lax.axis_index("narrow")]
    scale = lax.rsqrt(jnp.mean(routed * routed, axis=1, keepdims=True) + EPSILON)
    normed = (routed * scale * gain_ref[...]).astype(BF16)
    normed_ref[...] = normed
    channel_in = dot_nt(normed, in_w_ref[...])[:rows]
    heads = dot_nt(normed, heads_w_ref[...])[:rows].astype(BF16).astype(F32)
    channel_ref[...] = channel_in
    conv_out = base_ref[:rows] + base_ref[rows:] * channel_in
    act = conv_out * sigmoid(conv_out)
    act_ref[...] = act
    state = dot_nt(act.astype(BF16), xproj_ref[...])
    part_ref[...] = jnp.concatenate([heads, state], axis=1)


def project_gate(normed_ref, gate_w_ref, channel_ref, old_conv_ref, gate_ref, new_conv_ref):
    taps = new_conv_ref.shape[0]
    for tap in range(taps - 1):
        new_conv_ref[tap] = old_conv_ref[tap]
    new_conv_ref[taps - 1] = channel_ref[...].astype(BF16)
    gate = dot_nt(normed_ref[...], gate_w_ref[1])[: gate_ref.shape[0]]
    gate_ref[...] = gate * sigmoid(gate)


def state_step(kv_ref, *refs, size, head_width):
    pieces = refs[:size]
    (act_ref, gate_ref, dt_w_ref, dt_b_ref, a_log_ref, ssm_ref, skip_ref, out_w_ref, part_ref,
     new_ssm_ref, new_kv_ref) = refs[size:]
    new_kv_ref[...] = kv_ref[...].astype(BF16)
    state = pieces[0][:, head_width:]
    for piece in pieces[1:]:
        state = state + piece[:, head_width:]
    rows = state.shape[0]
    rank = dt_w_ref.shape[1]
    depth = a_log_ref.shape[0]
    step = dot_nt(state[:, :rank].astype(BF16), dt_w_ref[...]) + dt_b_ref[...]
    step = jnp.maximum(step, 0.0) + jnp.log1p(jnp.exp(-jnp.abs(step)))
    act = act_ref[...]
    rates = jnp.exp(a_log_ref[...])
    maps = jnp.concatenate(
        [state[:, rank:], jnp.zeros((rows, 128 - 2 * depth), F32)], axis=1
    )
    maps = jnp.concatenate([maps, jnp.zeros((8 - rows, 128), F32)], axis=0).T
    outs = []
    for r in range(rows):
        step_row = step[r : r + 1]
        fresh = jnp.exp(-step_row * rates) * ssm_ref[r] + maps[:depth, r : r + 1] * (
            step_row * act[r : r + 1]
        )
        new_ssm_ref[r] = fresh
        outs.append(jnp.sum(maps[depth : 2 * depth, r : r + 1] * fresh, axis=0, keepdims=True))
    state_out = jnp.concatenate(outs, axis=0) + skip_ref[...] * act
    ssm_heads = (state_out * gate_ref[...]).astype(BF16)
    part_ref[...] = jnp.dot(ssm_heads, out_w_ref[...], preferred_element_type=F32).astype(BF16)


def attend(*refs, size, head_width):
    pieces = refs[:size]
    (live_ref, keys_ref, values_ref, part_ref, new_kv_ref, held) = refs[size:]
    me = lax.axis_index("narrow")
    stack_pieces(me, pieces, held)
    rows = held.shape[1]
    heads = jnp.concatenate([held[i][:, :head_width] for i in range(size)], axis=1)
    new_kv_ref[...] = heads[:, QUERY_WIDTH:]
    tall = jnp.concatenate([heads, jnp.zeros((8 - rows, heads.shape[1]), F32)], axis=0)
    tall = jnp.concatenate([tall, jnp.zeros((8, -tall.shape[1] % 128), F32)], axis=1)
    lane = lax.broadcasted_iota(jnp.int32, (8, 128), 1)
    row = lax.broadcasted_iota(jnp.int32, (8, 128), 0)
    first = lane < HEAD_SIZE

    turned = {}

    def twice(at):
        tile = at // 128
        if tile not in turned:
            line = tall[:, tile * 128 : tile * 128 + 128]
            turned[tile] = (line, pltpu.roll(line, HEAD_SIZE, 1))
        line, other = turned[tile]
        return jnp.where(first, line, other) if at % 128 == 0 else jnp.where(first, other, line)

    blocks = -(-rows // 2)
    own_block = [
        jnp.where(row == jnp.where(first, 2 * i, 2 * i + 1), 1.0, 0.0) for i in range(blocks)
    ]
    half = jnp.where(first, HEAD_SIZE ** -0.5, 0.0)
    groups = range(KEY_VALUE_HEADS)
    queries = [[twice(j * HEAD_SIZE) for j in range(g * GROUP, (g + 1) * GROUP)] for g in groups]
    scores = []
    for g in groups:
        spread = jnp.concatenate(
            [
                jnp.concatenate([q * (HEAD_SIZE ** -0.5) * mask for mask in own_block], axis=1)
                for q in queries[g]
            ],
            axis=0,
        ).astype(BF16)
        keys = jnp.concatenate(
            [keys_ref[r, g * HEAD_SIZE : (g + 1) * HEAD_SIZE, :] for r in range(rows)], axis=0
        )
        scores.append(jnp.dot(spread, keys, preferred_element_type=F32))
    new_keys = [twice(QUERY_WIDTH + g * HEAD_SIZE) * half for g in groups]
    own = [
        jnp.sum(
            jnp.concatenate([q * new_keys[g] for q in queries[g]], axis=0), axis=1, keepdims=True
        )
        for g in groups
    ]

    live = jnp.concatenate([live_ref[...]] * GROUP, axis=0) > 0.0
    tops = [
        jnp.maximum(
            jnp.max(jnp.where(live, scores[g], -jnp.inf), axis=1, keepdims=True), own[g]
        )
        for g in groups
    ]
    weights = [
        jnp.where(live, jnp.exp(scores[g] - tops[g]), 0.0).astype(BF16) for g in groups
    ]
    own_here = jnp.where(me == 0, 1.0, 0.0)
    own_weights = [
        jnp.exp(own[g] - tops[g]).astype(BF16).astype(F32) * own_here for g in groups
    ]
    products = []
    for g in groups:
        values = jnp.concatenate(
            [values_ref[r, g * HEAD_SIZE : (g + 1) * HEAD_SIZE, :] for r in range(rows)], axis=0
        )
        products.append(dot_nt(weights[g], values))
    totals = [
        jnp.sum(weights[g].astype(F32), axis=1, keepdims=True) + own_weights[g] for g in groups
    ]
    stats = jnp.zeros((8, 128), F32)
    numers = []
    for g in groups:
        new_value = twice(QUERY_WIDTH + KEY_VALUE_WIDTH + g * HEAD_SIZE)
        for k in range(GROUP):
            j = g * GROUP + k
            at = slice(8 * k, 8 * k + 8)
            folded = products[g][at, :128] * own_block[0]
            for i in range(1, blocks):
                folded = folded + products[g][at, 128 * i : 128 * i + 128] * own_block[i]
            numers.append(
                folded + pltpu.roll(folded, HEAD_SIZE, 1) + own_weights[g][at] * new_value
            )
            stats = jnp.where(lane == j, tops[g][at], stats)
            stats = jnp.where(lane == QUERY_HEADS + j, totals[g][at], stats)
    lines = [
        jnp.where(first, numers[j], numers[j + 1]) for j in range(0, QUERY_HEADS - 1, 2)
    ]
    high = stats.astype(BF16).astype(F32)
    middle = (stats - high).astype(BF16).astype(F32)
    low = stats - high - middle
    lines.append(jnp.where(first, numers[-1], pltpu.roll(high, HEAD_SIZE, 1)))
    lines.append(jnp.where(first, middle, pltpu.roll(low, HEAD_SIZE, 1)))
    part_ref[...] = jnp.concatenate(lines, axis=1)[:rows].astype(BF16)


def project_out(*refs, size):
    pieces = refs[:size]
    (state_ref, spread_ref, w_ref, y_ref, part_ref) = refs[size:]
    rows = y_ref.shape[0]
    stats = [
        functools.reduce(
            jnp.add,
            [
                p[:, QUERY_WIDTH + i * HEAD_SIZE : QUERY_WIDTH + (i + 1) * HEAD_SIZE].astype(F32)
                for i in range(3)
            ],
        )
        for p in pieces
    ]
    tops = [t[:, :QUERY_HEADS] for t in stats]
    totals = [t[:, QUERY_HEADS : 2 * QUERY_HEADS] for t in stats]
    top = functools.reduce(jnp.maximum, tops)
    factors = [jnp.exp(t - top) for t in tops]
    total = functools.reduce(jnp.add, [f * t for f, t in zip(factors, totals)])
    factors = jnp.concatenate([f / total for f in factors], axis=0)
    high = factors.astype(BF16)
    low = (factors - high.astype(F32)).astype(BF16)
    spread = jnp.dot(high, spread_ref[...], preferred_element_type=F32) + jnp.dot(
        low, spread_ref[...], preferred_element_type=F32
    )
    merged = functools.reduce(
        jnp.add,
        [spread[i * rows : (i + 1) * rows] * p[:, :QUERY_WIDTH].astype(F32) for i, p in enumerate(pieces)],
    )
    y_attn = dot_nt(merged.astype(BF16), w_ref[...])
    y_ref[...] = y_attn
    square = jnp.sum(y_attn * y_attn, axis=1, keepdims=True)
    high = square.astype(BF16)
    rest = square - high.astype(F32)
    low = rest.astype(BF16)
    lowest = (rest - low.astype(F32)).astype(BF16)
    part_ref[...] = jnp.concatenate(
        [state_ref[...], high, low, lowest, jnp.zeros((rows, part_ref.shape[1] - MODEL_WIDTH - 3), BF16)],
        axis=1,
    )


def finish(*refs, size):
    pieces = refs[:size]
    y_ref, cols_ref, gain_attn_ref, gain_ssm_ref, out_ref, blocks = refs[size:]
    cols = out_ref.shape[1]
    total = functools.reduce(jnp.add, [p[...].astype(F32) for p in pieces])
    square = jnp.sum(total[:, MODEL_WIDTH : MODEL_WIDTH + 3], axis=1, keepdims=True)
    attn_scale = lax.rsqrt(square / MODEL_WIDTH + EPSILON)
    y_ssm = total[:, :MODEL_WIDTH]
    state_scale = lax.rsqrt(jnp.mean(y_ssm * y_ssm, axis=1, keepdims=True) + EPSILON)
    for block in range(blocks.shape[0]):
        blocks[block] = y_ssm[:, block * cols : (block + 1) * cols]
    mixed = 0.5 * (
        y_ref[...] * attn_scale * gain_attn_ref[...]
        + blocks[lax.axis_index("narrow")] * state_scale * gain_ssm_ref[...]
    )
    out_ref[...] = (cols_ref[...] + mixed).astype(BF16)


SMEM = pl.BlockSpec(memory_space=pltpu.SMEM)
VMEM = pl.BlockSpec(memory_space=pltpu.VMEM)


def call(body, scalars, blocks, outs, scratch=(), after=()):
    def run(*refs):
        body(*refs[len(after) :])

    return pl.pallas_call(
        run,
        in_specs=[pl.BlockSpec(memory_space=pl.ANY)] * len(after)
        + [SMEM] * len(scalars)
        + [VMEM] * len(blocks),
        out_specs=[VMEM] * len(outs),
        out_shape=outs,
        scratch_shapes=scratch,
        compiler_params=pltpu.CompilerParams(vmem_limit_bytes=16 * 1024 * 1024),
    )(*after, *scalars, *blocks)


def shards(
    tokens,
    source,
    lengths,
    cached_key_rows,
    cached_value_rows,
    conv_state,
    ssm_state,
    norm_gain,
    query_key_value_weight,
    w_xz,
    conv_weight,
    conv_bias,
    w_xproj,
    w_dt,
    dt_bias,
    a_log,
    skip_d,
    w_attn_out,
    w_ssm_out,
    gain_attn,
    gain_ssm,
):
    rows = tokens.shape[0]
    narrow = lax.axis_size("narrow")
    cols = MODEL_WIDTH // narrow
    head_width = query_key_value_weight.shape[1]
    shape = jax.ShapeDtypeStruct

    wide = lax.axis_size("wide")
    large = (query_key_value_weight.T, w_xproj.T, w_xz.transpose(1, 2, 0))
    small = (source, lengths, norm_gain, conv_weight, conv_bias[None], conv_state.transpose(1, 0, 2))
    slots = rows * entries_of(wide)
    half = large[2].shape[1:]
    pinned = [pltpu.with_memory_space_constraint(a, pltpu.HBM) for a in small + large]
    anywhere = pl.BlockSpec(memory_space=pl.ANY)
    prepared = pl.pallas_call(
        functools.partial(prepare, size=wide),
        in_specs=[anywhere] * len(pinned),
        out_specs=[VMEM] * 8,
        out_shape=[
            pltpu.VMEM((8, slots), F32),
            pltpu.VMEM((8, cached_key_rows.shape[1]), F32),
            pltpu.VMEM((2 * rows, cols), F32),
            pltpu.VMEM(small[5].shape, BF16),
            pltpu.VMEM((1, MODEL_WIDTH), F32),
            pltpu.VMEM(large[0].shape, BF16),
            pltpu.VMEM(large[1].shape, BF16),
            pltpu.VMEM(half, BF16),
        ],
        scratch_shapes=[pltpu.SMEM(a.shape, jnp.int32) for a in small[:2]]
        + [pltpu.VMEM(a.shape, a.dtype) for a in small[2:]]
        + [pltpu.SemaphoreType.DMA((7 + 2 * (PARTS + 1),))],
        compiler_params=pltpu.CompilerParams(vmem_limit_bytes=4 * 1024 * 1024),
    )(*pinned)
    arrived = gather_xor(tokens, "wide", "narrow", prepared[:1])
    part_width = head_width + w_xproj.shape[1]
    chosen, live, base, old_conv, *weights = prepared
    part, act, normed, channel_in, routed_cols = call(
        functools.partial(project_in, size=len(arrived)),
        (),
        (*arrived, chosen, base, *weights),
        (
            shape((rows, part_width), F32),
            shape((rows, cols), F32),
            shape((8, MODEL_WIDTH), BF16),
            shape((rows, cols), F32),
            shape((rows, cols), F32),
        ),
        (pltpu.VMEM((narrow, rows, cols), F32),),
    )
    pieces = exchange(part, "narrow")
    gate, new_conv = call(
        project_gate,
        (),
        (normed, w_xz.transpose(1, 2, 0), channel_in, old_conv),
        (shape((rows, cols), F32), shape(old_conv.shape, BF16)),
    )
    second, key_value = call(
        functools.partial(attend, size=narrow, head_width=head_width),
        (),
        (*pieces, live, cached_key_rows.transpose(0, 2, 1), cached_value_rows.transpose(0, 2, 1)),
        (
            shape((rows, QUERY_WIDTH + 3 * HEAD_SIZE), BF16),
            shape((rows, 2 * KEY_VALUE_WIDTH), F32),
        ),
        (pltpu.VMEM((narrow, rows, part_width), F32),),
        after=(gate,),
    )
    state_part, new_ssm, new_kv = call(
        functools.partial(state_step, size=narrow, head_width=head_width),
        (),
        (
            key_value, *pieces, act, gate, w_dt.T, dt_bias[None], a_log, ssm_state, skip_d[None], w_ssm_out,
        ),
        (
            shape((rows, MODEL_WIDTH), BF16),
            shape(ssm_state.shape, F32),
            shape(key_value.shape, BF16),
        ),
    )
    pieces = exchange(second, "narrow")
    pieces = [pieces[0]] + [pieces[k] for k in (2, 3, 1)]
    spread = (
        lax.broadcasted_iota(jnp.int32, (QUERY_HEADS, QUERY_WIDTH), 1) // HEAD_SIZE
        == lax.broadcasted_iota(jnp.int32, (QUERY_HEADS, QUERY_WIDTH), 0)
    ).astype(BF16)
    y_attn, third = call(
        functools.partial(project_out, size=narrow),
        (),
        (*pieces, state_part, spread, w_attn_out.T),
        (shape((rows, cols), F32), shape((rows, MODEL_WIDTH + 64), BF16)),
    )
    pieces = exchange(third, "narrow")
    (out,) = call(
        functools.partial(finish, size=narrow),
        (),
        (*pieces, y_attn, routed_cols, gain_attn[None], gain_ssm[None]),
        (shape((rows, cols), BF16),),
        (pltpu.VMEM((narrow, rows, cols), F32),),
    )
    return (out, new_kv, new_conv.transpose(1, 0, 2), new_ssm)


def solution(mesh):
    placed = (
        P("wide", None),
        P("wide"),
        P("wide"),
        P("wide", "narrow", None),
        P("wide", "narrow", None),
        P("wide", None, "narrow"),
        P("wide", None, "narrow"),
        P(),
        P(None, "narrow"),
        P(None, None, "narrow"),
        P(None, "narrow"),
        P("narrow"),
        P("narrow", None),
        P(None, "narrow"),
        P("narrow"),
        P(None, "narrow"),
        P("narrow"),
        P(None, "narrow"),
        P("narrow", None),
        P("narrow"),
        P("narrow"),
    )
    return jax.shard_map(
        shards,
        mesh=mesh,
        in_specs=placed,
        out_specs=(
            P("wide", "narrow"),
            P("wide", None),
            P("wide", None, "narrow"),
            P("wide", None, "narrow"),
        ),
        check_vma=False,
    )
```

```python
import functools
import jax
import jax.numpy as jnp
from jax import lax
from jax.experimental import pallas as pl
from jax.experimental.pallas import tpu as pltpu
from jax.sharding import PartitionSpec as P

MODEL_WIDTH = 1600
QUERY_HEADS = 25
KEY_VALUE_HEADS = 5
HEAD_SIZE = 64
WINDOW_LENGTH = 1024
GROUP = QUERY_HEADS // KEY_VALUE_HEADS
QUERY_WIDTH = QUERY_HEADS * HEAD_SIZE
KEY_VALUE_WIDTH = KEY_VALUE_HEADS * HEAD_SIZE


EPSILON = 1e-06
PARTS = 4

NT = (((1,), (1,)), ((), ()))
F32 = jnp.float32
BF16 = jnp.bfloat16


def dot_nt(a, b):
    return lax.dot_general(a, b, NT, preferred_element_type=F32)


def sigmoid(v):
    return 1.0 / (1.0 + jnp.exp(-v))


def exchange(part, order):
    return [part] + [swap(part, step) for step in order]


def join(*refs):
    *given, out_ref = refs
    at = 0
    for ref in given:
        out_ref[at : at + ref.shape[0]] = ref[...]
        at += ref.shape[0]


def swap(part, step):
    size = lax.axis_size("narrow")
    assert size == 4
    return lax.ppermute(part, "narrow", [(i, i ^ step) for i in range(size)])


def digits_of(size):
    assert size & (size - 1) == 0
    rounds, done, total = [], 0, size.bit_length() - 1
    while done < total:
        count = 1 if (total - done) % 2 else 2
        rounds.append((done, count))
        done += count
    return rounds


def gather_xor(part, axis, core_axis, beside):
    size, cores = lax.axis_size(axis), lax.axis_size(core_axis)
    blocks = [part[None]]
    rounds = digits_of(size)
    for place, count in rounds:
        held = blocks[0]
        if len(blocks) > 1:
            entries = sum(b.shape[0] for b in blocks)
            (held,) = call(
                join, (), blocks, (jax.ShapeDtypeStruct((entries, *part.shape), part.dtype),), after=beside
            )
            beside = ()
        if count == 2 and place == rounds[-1][0]:

            def fetch(even, odd):
                moves = [
                    (i * cores + c, (i ^ (step << place)) * cores + c)
                    for i in range(size)
                    for c in range(cores)
                    for step in [odd if c % 2 else even]
                    if step
                ]
                return lax.ppermute(held, (axis, core_axis), moves)

            far, near = fetch(3, 2), fetch(0, 1)
            near_swap = lax.ppermute(near, core_axis, [(c, c - 1) for c in range(1, cores, 2)])
            far_swap = lax.ppermute(far, core_axis, [(c, c ^ 1) for c in range(cores)])
            blocks = [held, near, near_swap, far, far_swap]
        else:
            blocks = [held] + [
                lax.ppermute(held, axis, [(i, i ^ (step << place)) for i in range(size)])
                for step in range((1 << count) - 1, 0, -1)
            ]
    return blocks


def entries_of(size):
    rounds = digits_of(size)
    return (5 * size) // 4 if rounds[-1][1] == 2 else size


def entry_of(away, size, core):
    entry, done = jnp.int32(0), 0
    rounds = digits_of(size)
    for place, count in rounds:
        top = (1 << count) - 1
        digit = lax.bitwise_and(lax.shift_right_logical(away, place), top)
        if count == 2 and place == rounds[-1][0]:
            odd = lax.bitwise_and(core, 1)
            near = 2 - odd
            far = jnp.where(digit == 3 - odd, 3, 4)
            block = jnp.where(digit == 0, 0, jnp.where(digit == 1, near, far))
        else:
            block = lax.bitwise_and(top + 1 - digit, top)
        entry = entry + block * (1 << done)
        done += count
    return entry


def cut(rows, count):
    step = -(-rows // (16 * count)) * 16
    return [(at, min(step, rows - at)) for at in range(0, rows, step)]


def copies_of(pairs, sems):
    copies = []
    for origin, to in pairs:
        if len(to.shape) == 2 and to.shape[0] >= 256:
            ranges = [pl.ds(at, size) for at, size in cut(to.shape[0], PARTS)]
            copies += [(origin.at[r], to.at[r]) for r in ranges]
        else:
            copies.append((origin, to))
    return [pltpu.make_async_copy(origin, to, sems.at[i]) for i, (origin, to) in enumerate(copies)]


def live_slots(lengths, span, me):
    row_id = lax.broadcasted_iota(jnp.int32, (8, span), 0)
    slot = lax.broadcasted_iota(jnp.int32, (8, span), 1) + me * span
    length = jnp.zeros((8, span), jnp.int32)
    hole = jnp.zeros((8, span), jnp.int32)
    for r in range(lengths.shape[0]):
        count = lengths[r]
        length = jnp.where(row_id == r, count, length)
        hole = jnp.where(
            row_id == r, jnp.where(count >= WINDOW_LENGTH, lax.rem(count, WINDOW_LENGTH), -1), hole
        )
    return jnp.where((slot < length) & (slot != hole), 1.0, 0.0)


def prepare(
    source_ref, lengths_ref, gain_ref, conv_w_ref, conv_b_ref, conv_rows_ref, heads_ref, xproj_ref, xz_ref,
    chosen_ref, live_ref, base_ref, new_conv_ref, gain_out, heads_out, xproj_out, in_out,
    source, lengths, gain, conv_w, conv_b, conv_rows, sems, *, size,
):
    rows = source.shape[0]
    small = (
        (source_ref, source), (lengths_ref, lengths), (gain_ref, gain), (conv_w_ref, conv_w), (conv_b_ref, conv_b),
        (conv_rows_ref, conv_rows),
    )
    copies = copies_of(
        small + ((heads_ref, heads_out), (xz_ref.at[0], in_out), (xproj_ref, xproj_out)), sems
    )
    for copy in copies:
        copy.start()
    for copy in copies[: len(small)]:
        copy.wait()
    me = lax.axis_index("narrow")
    slots = chosen_ref.shape[1]
    row_id = lax.broadcasted_iota(jnp.int32, (8, slots), 0)
    wanted = jnp.full((8, slots), -1, jnp.int32)
    for r in range(rows):
        away = lax.bitwise_xor(lax.div(source[r], rows), lax.axis_index("wide"))
        entry = entry_of(away, size, me)
        wanted = jnp.where(row_id == r, entry * rows + lax.rem(source[r], rows), wanted)
    chosen = lax.broadcasted_iota(jnp.int32, (8, slots), 1) == wanted
    chosen_ref[...] = jnp.where(chosen, 1.0, 0.0)
    live_ref[...] = live_slots(lengths, live_ref.shape[1], me)
    gain_out[...] = gain[...][None]
    taps = conv_rows.shape[0]
    base = conv_b[...]
    for tap in range(taps):
        base = base + conv_w[tap : tap + 1] * conv_rows[tap].astype(F32)
    base_ref[:rows] = base
    base_ref[rows:] = jnp.broadcast_to(conv_w[taps:], base.shape)
    for tap in range(taps - 1):
        new_conv_ref[tap] = conv_rows[tap + 1]
    new_conv_ref[taps - 1] = jnp.zeros_like(conv_rows[0])
    for copy in copies[len(small) :]:
        copy.wait()


def project_in(*refs, size):
    arrived_refs = refs[:size]
    (other_w_ref, chosen_ref, base_ref, gain_ref, heads_w_ref, xproj_ref, in_w_ref, part_ref,
     state_ref, act_ref, normed_ref, channel_ref, cols_ref, blocks) = refs[size:]
    rows, cols = cols_ref.shape
    arrived = jnp.concatenate(
        [ref[i].astype(F32) for ref in arrived_refs for i in range(ref.shape[0])], axis=0
    ).astype(BF16)
    routed = jnp.dot(chosen_ref[...].astype(BF16), arrived, preferred_element_type=F32)
    for block in range(blocks.shape[0]):
        blocks[block] = routed[:rows, block * cols : (block + 1) * cols]
    cols_ref[...] = blocks[lax.axis_index("narrow")]
    scale = lax.rsqrt(jnp.mean(routed * routed, axis=1, keepdims=True) + EPSILON)
    normed = (routed * scale * gain_ref[...]).astype(BF16)
    normed_ref[...] = normed
    channel_in = dot_nt(normed, in_w_ref[...])[:rows]
    heads = [
        dot_nt(normed, w[...])[:rows].astype(BF16).astype(F32) for w in (heads_w_ref, other_w_ref)
    ]
    channel_ref[...] = channel_in
    conv_out = base_ref[:rows] + base_ref[rows:] * channel_in
    act = conv_out * sigmoid(conv_out)
    act_ref[...] = act
    state = dot_nt(act.astype(BF16), xproj_ref[...])
    state_ref[...] = state
    part_ref[...] = jnp.concatenate([*heads, state], axis=1)


def keep_conv(channel_ref, old_conv_ref, new_conv_ref):
    taps = new_conv_ref.shape[0]
    for tap in range(taps - 1):
        new_conv_ref[tap] = old_conv_ref[tap]
    new_conv_ref[taps - 1] = channel_ref[...].astype(BF16)


def state_step(
    kv_ref, far_ref, *refs, size,
):
    states = refs[: size - 1]
    (normed_ref, gate_w_ref, act_ref, dt_w_ref, dt_b_ref, a_log_ref, ssm_ref, skip_ref, out_w_ref,
     part_ref, new_ssm_ref, new_kv_ref) = refs[size - 1 :]
    new_kv_ref[...] = kv_ref[...].astype(BF16)
    state = far_ref[:, far_ref.shape[1] - states[0].shape[1] :]
    for other in states:
        state = state + other[...]
    rows = state.shape[0]
    gate = dot_nt(normed_ref[...], gate_w_ref[1])[:rows]
    rank = dt_w_ref.shape[1]
    depth = a_log_ref.shape[0]
    step = dot_nt(state[:, :rank].astype(BF16), dt_w_ref[...]) + dt_b_ref[...]
    step = jnp.maximum(step, 0.0) + jnp.log1p(jnp.exp(-jnp.abs(step)))
    act = act_ref[...]
    rates = jnp.exp(a_log_ref[...])
    maps = jnp.concatenate(
        [state[:, rank:], jnp.zeros((rows, 128 - 2 * depth), F32)], axis=1
    )
    maps = jnp.concatenate([maps, jnp.zeros((8 - rows, 128), F32)], axis=0).T
    outs = []
    for r in range(rows):
        step_row = step[r : r + 1]
        fresh = jnp.exp(-step_row * rates) * ssm_ref[r] + maps[:depth, r : r + 1] * (
            step_row * act[r : r + 1]
        )
        new_ssm_ref[r] = fresh
        outs.append(jnp.sum(maps[depth : 2 * depth, r : r + 1] * fresh, axis=0, keepdims=True))
    state_out = jnp.concatenate(outs, axis=0) + skip_ref[...] * act
    ssm_heads = (state_out * (gate * sigmoid(gate))).astype(BF16)
    part_ref[...] = jnp.dot(ssm_heads, out_w_ref[...], preferred_element_type=F32).astype(BF16)


def attend(
    near_ref, far_ref, live_ref, keys_ref, values_ref, part_ref, new_kv_ref, held, *, head_width
):
    me = lax.axis_index("narrow")
    rows = held.shape[1]
    for step in range(held.shape[0]):
        piece = far_ref if step & 2 else near_ref
        at = (step & 1) * head_width
        held[lax.bitwise_xor(me, step)] = piece[:, at : at + head_width]
    heads = jnp.concatenate([held[i] for i in range(held.shape[0])], axis=1)
    new_kv_ref[...] = heads[:, QUERY_WIDTH:]
    tall = jnp.concatenate([heads, jnp.zeros((8 - rows, heads.shape[1]), F32)], axis=0)
    tall = jnp.concatenate([tall, jnp.zeros((8, -tall.shape[1] % 128), F32)], axis=1)
    lane = lax.broadcasted_iota(jnp.int32, (8, 128), 1)
    row = lax.broadcasted_iota(jnp.int32, (8, 128), 0)
    first = lane < HEAD_SIZE

    turned = {}

    def twice(at):
        tile = at // 128
        if tile not in turned:
            line = tall[:, tile * 128 : tile * 128 + 128]
            turned[tile] = (line, pltpu.roll(line, HEAD_SIZE, 1))
        line, other = turned[tile]
        return jnp.where(first, line, other) if at % 128 == 0 else jnp.where(first, other, line)

    blocks = -(-rows // 2)
    own_block = [
        jnp.where(row == jnp.where(first, 2 * i, 2 * i + 1), 1.0, 0.0) for i in range(blocks)
    ]
    half = jnp.where(first, HEAD_SIZE ** -0.5, 0.0)
    groups = range(KEY_VALUE_HEADS)
    queries = [[twice(j * HEAD_SIZE) for j in range(g * GROUP, (g + 1) * GROUP)] for g in groups]
    scores = []
    for g in groups:
        spread = jnp.concatenate(
            [
                jnp.concatenate([q * (HEAD_SIZE ** -0.5) * mask for mask in own_block], axis=1)
                for q in queries[g]
            ],
            axis=0,
        ).astype(BF16)
        keys = jnp.concatenate(
            [keys_ref[r, g * HEAD_SIZE : (g + 1) * HEAD_SIZE, :] for r in range(rows)], axis=0
        )
        scores.append(jnp.dot(spread, keys, preferred_element_type=F32))
    new_keys = [twice(QUERY_WIDTH + g * HEAD_SIZE) * half for g in groups]
    own = [
        jnp.sum(
            jnp.concatenate([q * new_keys[g] for q in queries[g]], axis=0), axis=1, keepdims=True
        )
        for g in groups
    ]

    live = jnp.concatenate([live_ref[...]] * GROUP, axis=0) > 0.0
    tops = [
        jnp.maximum(
            jnp.max(jnp.where(live, scores[g], -jnp.inf), axis=1, keepdims=True), own[g]
        )
        for g in groups
    ]
    weights = [
        jnp.where(live, jnp.exp(scores[g] - tops[g]), 0.0).astype(BF16) for g in groups
    ]
    own_here = jnp.where(me == 0, 1.0, 0.0)
    own_weights = [
        jnp.exp(own[g] - tops[g]).astype(BF16).astype(F32) * own_here for g in groups
    ]
    products = []
    for g in groups:
        values = jnp.concatenate(
            [values_ref[r, g * HEAD_SIZE : (g + 1) * HEAD_SIZE, :] for r in range(rows)], axis=0
        )
        products.append(dot_nt(weights[g], values))
    totals = [
        jnp.sum(weights[g].astype(F32), axis=1, keepdims=True) + own_weights[g] for g in groups
    ]
    stats = jnp.zeros((8, 128), F32)
    numers = []
    for g in groups:
        new_value = twice(QUERY_WIDTH + KEY_VALUE_WIDTH + g * HEAD_SIZE)
        for k in range(GROUP):
            j = g * GROUP + k
            at = slice(8 * k, 8 * k + 8)
            folded = products[g][at, :128] * own_block[0]
            for i in range(1, blocks):
                folded = folded + products[g][at, 128 * i : 128 * i + 128] * own_block[i]
            numers.append(
                folded + pltpu.roll(folded, HEAD_SIZE, 1) + own_weights[g][at] * new_value
            )
            stats = jnp.where(lane == j, tops[g][at], stats)
            stats = jnp.where(lane == QUERY_HEADS + j, totals[g][at], stats)
    lines = [
        jnp.where(first, numers[j], numers[j + 1]) for j in range(0, QUERY_HEADS - 1, 2)
    ]
    high = stats.astype(BF16).astype(F32)
    middle = (stats - high).astype(BF16).astype(F32)
    low = stats - high - middle
    lines.append(jnp.where(first, numers[-1], pltpu.roll(high, HEAD_SIZE, 1)))
    lines.append(jnp.where(first, middle, pltpu.roll(low, HEAD_SIZE, 1)))
    part_ref[...] = jnp.concatenate(lines, axis=1)[:rows].astype(BF16)


def project_out(*refs, size):
    pieces = refs[:size]
    (state_ref, spread_ref, w_ref, y_ref, part_ref) = refs[size:]
    rows = y_ref.shape[0]
    stats = [
        functools.reduce(
            jnp.add,
            [
                p[:, QUERY_WIDTH + i * HEAD_SIZE : QUERY_WIDTH + (i + 1) * HEAD_SIZE].astype(F32)
                for i in range(3)
            ],
        )
        for p in pieces
    ]
    tops = [t[:, :QUERY_HEADS] for t in stats]
    totals = [t[:, QUERY_HEADS : 2 * QUERY_HEADS] for t in stats]
    top = functools.reduce(jnp.maximum, tops)
    factors = [jnp.exp(t - top) for t in tops]
    total = functools.reduce(jnp.add, [f * t for f, t in zip(factors, totals)])
    factors = jnp.concatenate([f / total for f in factors], axis=0)
    high = factors.astype(BF16)
    low = (factors - high.astype(F32)).astype(BF16)
    spread = jnp.dot(high, spread_ref[...], preferred_element_type=F32) + jnp.dot(
        low, spread_ref[...], preferred_element_type=F32
    )
    merged = functools.reduce(
        jnp.add,
        [spread[i * rows : (i + 1) * rows] * p[:, :QUERY_WIDTH].astype(F32) for i, p in enumerate(pieces)],
    )
    y_attn = dot_nt(merged.astype(BF16), w_ref[...])
    y_ref[...] = y_attn
    square = jnp.sum(y_attn * y_attn, axis=1, keepdims=True)
    high = square.astype(BF16)
    rest = square - high.astype(F32)
    low = rest.astype(BF16)
    lowest = (rest - low.astype(F32)).astype(BF16)
    part_ref[...] = jnp.concatenate(
        [state_ref[...], high, low, lowest, jnp.zeros((rows, part_ref.shape[1] - MODEL_WIDTH - 3), BF16)],
        axis=1,
    )


def finish(*refs, size):
    pieces = refs[:size]
    y_ref, cols_ref, gain_attn_ref, gain_ssm_ref, out_ref, blocks = refs[size:]
    cols = out_ref.shape[1]
    total = functools.reduce(jnp.add, [p[...].astype(F32) for p in pieces])
    square = jnp.sum(total[:, MODEL_WIDTH : MODEL_WIDTH + 3], axis=1, keepdims=True)
    attn_scale = lax.rsqrt(square / MODEL_WIDTH + EPSILON)
    y_ssm = total[:, :MODEL_WIDTH]
    state_scale = lax.rsqrt(jnp.mean(y_ssm * y_ssm, axis=1, keepdims=True) + EPSILON)
    for block in range(blocks.shape[0]):
        blocks[block] = y_ssm[:, block * cols : (block + 1) * cols]
    mixed = 0.5 * (
        y_ref[...] * attn_scale * gain_attn_ref[...]
        + blocks[lax.axis_index("narrow")] * state_scale * gain_ssm_ref[...]
    )
    out_ref[...] = (cols_ref[...] + mixed).astype(BF16)


SMEM = pl.BlockSpec(memory_space=pltpu.SMEM)
VMEM = pl.BlockSpec(memory_space=pltpu.VMEM)


def call(body, scalars, blocks, outs, scratch=(), after=()):
    def run(*refs):
        body(*refs[len(after) :])

    return pl.pallas_call(
        run,
        in_specs=[pl.BlockSpec(memory_space=pl.ANY)] * len(after)
        + [SMEM] * len(scalars)
        + [VMEM] * len(blocks),
        out_specs=[VMEM] * len(outs),
        out_shape=outs,
        scratch_shapes=scratch,
        compiler_params=pltpu.CompilerParams(vmem_limit_bytes=16 * 1024 * 1024),
    )(*after, *scalars, *blocks)


def shards(
    tokens,
    source,
    lengths,
    cached_key_rows,
    cached_value_rows,
    conv_state,
    ssm_state,
    norm_gain,
    query_key_value_weight,
    w_xz,
    conv_weight,
    conv_bias,
    w_xproj,
    w_dt,
    dt_bias,
    a_log,
    skip_d,
    w_attn_out,
    w_ssm_out,
    gain_attn,
    gain_ssm,
):
    rows = tokens.shape[0]
    narrow = lax.axis_size("narrow")
    cols = MODEL_WIDTH // narrow
    head_width = query_key_value_weight.shape[1]
    shape = jax.ShapeDtypeStruct

    wide = lax.axis_size("wide")
    large = (query_key_value_weight.T, w_xproj.T, w_xz.transpose(1, 2, 0))
    small = (source, lengths, norm_gain, conv_weight, conv_bias[None], conv_state.transpose(1, 0, 2))
    slots = rows * entries_of(wide)
    half = large[2].shape[1:]
    pinned = [pltpu.with_memory_space_constraint(a, pltpu.HBM) for a in small + large]
    anywhere = pl.BlockSpec(memory_space=pl.ANY)
    prepared = pl.pallas_call(
        functools.partial(prepare, size=wide),
        in_specs=[anywhere] * len(pinned),
        out_specs=[VMEM] * 8,
        out_shape=[
            pltpu.VMEM((8, slots), F32),
            pltpu.VMEM((8, cached_key_rows.shape[1]), F32),
            pltpu.VMEM((2 * rows, cols), F32),
            pltpu.VMEM(small[5].shape, BF16),
            pltpu.VMEM((1, MODEL_WIDTH), F32),
            pltpu.VMEM(large[0].shape, BF16),
            pltpu.VMEM(large[1].shape, BF16),
            pltpu.VMEM(half, BF16),
        ],
        scratch_shapes=[pltpu.SMEM(a.shape, jnp.int32) for a in small[:2]]
        + [pltpu.VMEM(a.shape, a.dtype) for a in small[2:]]
        + [pltpu.SemaphoreType.DMA((7 + 2 * (PARTS + 1),))],
        compiler_params=pltpu.CompilerParams(vmem_limit_bytes=4 * 1024 * 1024),
    )(*pinned)
    arrived = gather_xor(tokens, "wide", "narrow", prepared[:1])
    other_w = swap(large[0], 1)
    part_width = 2 * head_width + w_xproj.shape[1]
    chosen, live, base, old_conv, *weights = prepared
    part, state, act, normed, channel_in, routed_cols = call(
        functools.partial(project_in, size=len(arrived)),
        (),
        (*arrived, other_w, chosen, base, *weights),
        (
            shape((rows, part_width), F32),
            shape((rows, w_xproj.shape[1]), F32),
            shape((rows, cols), F32),
            shape((8, MODEL_WIDTH), BF16),
            shape((rows, cols), F32),
            shape((rows, cols), F32),
        ),
        (pltpu.VMEM((narrow, rows, cols), F32),),
    )
    far = swap(part, 2)
    states = [state, swap(state, 1), swap(state, 3)]
    second, key_value = call(
        functools.partial(attend, head_width=head_width),
        (),
        (
            part, far, live, cached_key_rows.transpose(0, 2, 1),
            cached_value_rows.transpose(0, 2, 1),
        ),
        (
            shape((rows, QUERY_WIDTH + 3 * HEAD_SIZE), BF16),
            shape((rows, 2 * KEY_VALUE_WIDTH), F32),
        ),
        (pltpu.VMEM((narrow, rows, head_width), F32),),
    )
    state_part, new_ssm, new_kv = call(
        functools.partial(state_step, size=narrow),
        (),
        (
            key_value, far, *states, normed, w_xz.transpose(1, 2, 0), act, w_dt.T, dt_bias[None], a_log, ssm_state, skip_d[None], w_ssm_out,
        ),
        (
            shape((rows, MODEL_WIDTH), BF16),
            shape(ssm_state.shape, F32),
            shape(key_value.shape, BF16),
        ),
    )
    (new_conv,) = call(keep_conv, (), (channel_in, old_conv), (shape(old_conv.shape, BF16),))
    pieces = exchange(second, (3, 2, 1))
    spread = (
        lax.broadcasted_iota(jnp.int32, (QUERY_HEADS, QUERY_WIDTH), 1) // HEAD_SIZE
        == lax.broadcasted_iota(jnp.int32, (QUERY_HEADS, QUERY_WIDTH), 0)
    ).astype(BF16)
    y_attn, third = call(
        functools.partial(project_out, size=narrow),
        (),
        (*pieces, state_part, spread, w_attn_out.T),
        (shape((rows, cols), F32), shape((rows, MODEL_WIDTH + 64), BF16)),
    )
    pieces = exchange(third, (3, 2, 1))
    (out,) = call(
        functools.partial(finish, size=narrow),
        (),
        (*pieces, y_attn, routed_cols, gain_attn[None], gain_ssm[None]),
        (shape((rows, cols), BF16),),
        (pltpu.VMEM((narrow, rows, cols), F32),),
    )
    return (out, new_kv, new_conv.transpose(1, 0, 2), new_ssm)


def solution(mesh):
    placed = (
        P("wide", None),
        P("wide"),
        P("wide"),
        P("wide", "narrow", None),
        P("wide", "narrow", None),
        P("wide", None, "narrow"),
        P("wide", None, "narrow"),
        P(),
        P(None, "narrow"),
        P(None, None, "narrow"),
        P(None, "narrow"),
        P("narrow"),
        P("narrow", None),
        P(None, "narrow"),
        P("narrow"),
        P(None, "narrow"),
        P("narrow"),
        P(None, "narrow"),
        P("narrow", None),
        P("narrow"),
        P("narrow"),
    )
    return jax.shard_map(
        shards,
        mesh=mesh,
        in_specs=placed,
        out_specs=(
            P("wide", "narrow"),
            P("wide", None),
            P("wide", None, "narrow"),
            P("wide", None, "narrow"),
        ),
        check_vma=False,
    )
```

```python
import functools
import jax
import jax.numpy as jnp
from jax import lax
from jax.experimental import pallas as pl
from jax.experimental.pallas import tpu as pltpu
from jax.sharding import PartitionSpec as P

MODEL_WIDTH = 1600
QUERY_HEADS = 25
KEY_VALUE_HEADS = 5
HEAD_SIZE = 64
WINDOW_LENGTH = 1024
GROUP = QUERY_HEADS // KEY_VALUE_HEADS
QUERY_WIDTH = QUERY_HEADS * HEAD_SIZE
KEY_VALUE_WIDTH = KEY_VALUE_HEADS * HEAD_SIZE


EPSILON = 1e-06
PARTS = 4

NT = (((1,), (1,)), ((), ()))
F32 = jnp.float32
BF16 = jnp.bfloat16


def dot_nt(a, b):
    return lax.dot_general(a, b, NT, preferred_element_type=F32)


def sigmoid(v):
    return 1.0 / (1.0 + jnp.exp(-v))


def exchange(part, order):
    return [part] + [swap(part, step) for step in order]


def join(*refs):
    *given, out_ref = refs
    at = 0
    for ref in given:
        out_ref[at : at + ref.shape[0]] = ref[...]
        at += ref.shape[0]


def swap(part, step):
    size = lax.axis_size("narrow")
    assert size == 4
    return lax.ppermute(part, "narrow", [(i, i ^ step) for i in range(size)])


def digits_of(size):
    assert size & (size - 1) == 0
    rounds, done, total = [], 0, size.bit_length() - 1
    while done < total:
        count = 1 if (total - done) % 2 else 2
        rounds.append((done, count))
        done += count
    return rounds


def gather_xor(part, axis, core_axis, beside):
    size, cores = lax.axis_size(axis), lax.axis_size(core_axis)
    blocks = [part[None]]
    rounds = digits_of(size)
    for place, count in rounds:
        held = blocks[0]
        if len(blocks) > 1:
            entries = sum(b.shape[0] for b in blocks)
            (held,) = call(
                join, (), blocks, (jax.ShapeDtypeStruct((entries, *part.shape), part.dtype),), after=beside
            )
            beside = ()
        if count == 2 and place == rounds[-1][0]:

            def fetch(even, odd):
                moves = [
                    (i * cores + c, (i ^ (step << place)) * cores + c)
                    for i in range(size)
                    for c in range(cores)
                    for step in [odd if c % 2 else even]
                    if step
                ]
                return lax.ppermute(held, (axis, core_axis), moves)

            far, near = fetch(3, 2), fetch(0, 1)
            near_swap = lax.ppermute(near, core_axis, [(c, c - 1) for c in range(1, cores, 2)])
            far_swap = lax.ppermute(far, core_axis, [(c, c ^ 1) for c in range(cores)])
            blocks = [held, near, near_swap, far, far_swap]
        else:
            blocks = [held] + [
                lax.ppermute(held, axis, [(i, i ^ (step << place)) for i in range(size)])
                for step in range((1 << count) - 1, 0, -1)
            ]
    return blocks


def entries_of(size):
    rounds = digits_of(size)
    return (5 * size) // 4 if rounds[-1][1] == 2 else size


def entry_of(away, size, core):
    entry, done = jnp.int32(0), 0
    rounds = digits_of(size)
    for place, count in rounds:
        top = (1 << count) - 1
        digit = lax.bitwise_and(lax.shift_right_logical(away, place), top)
        if count == 2 and place == rounds[-1][0]:
            odd = lax.bitwise_and(core, 1)
            near = 2 - odd
            far = jnp.where(digit == 3 - odd, 3, 4)
            block = jnp.where(digit == 0, 0, jnp.where(digit == 1, near, far))
        else:
            block = lax.bitwise_and(top + 1 - digit, top)
        entry = entry + block * (1 << done)
        done += count
    return entry


def cut(rows, count):
    step = -(-rows // (16 * count)) * 16
    return [(at, min(step, rows - at)) for at in range(0, rows, step)]


def copies_of(pairs, sems):
    copies = []
    for origin, to in pairs:
        if len(to.shape) == 2 and to.shape[0] >= 256:
            ranges = [pl.ds(at, size) for at, size in cut(to.shape[0], PARTS)]
            copies += [(origin.at[r], to.at[r]) for r in ranges]
        else:
            copies.append((origin, to))
    return [pltpu.make_async_copy(origin, to, sems.at[i]) for i, (origin, to) in enumerate(copies)]


def live_slots(lengths, span, me):
    row_id = lax.broadcasted_iota(jnp.int32, (8, span), 0)
    slot = lax.broadcasted_iota(jnp.int32, (8, span), 1) + me * span
    length = jnp.zeros((8, span), jnp.int32)
    hole = jnp.zeros((8, span), jnp.int32)
    for r in range(lengths.shape[0]):
        count = lengths[r]
        length = jnp.where(row_id == r, count, length)
        hole = jnp.where(
            row_id == r, jnp.where(count >= WINDOW_LENGTH, lax.rem(count, WINDOW_LENGTH), -1), hole
        )
    return jnp.where((slot < length) & (slot != hole), 1.0, 0.0)


def prepare(
    source_ref, lengths_ref, gain_ref, conv_w_ref, conv_b_ref, conv_rows_ref, heads_ref, xproj_ref, xz_ref,
    chosen_ref, live_ref, base_ref, new_conv_ref, gain_out, heads_out, xproj_out, in_out,
    source, lengths, gain, conv_w, conv_b, conv_rows, sems, *, size,
):
    rows = source.shape[0]
    small = (
        (source_ref, source), (lengths_ref, lengths), (gain_ref, gain), (conv_w_ref, conv_w), (conv_b_ref, conv_b),
        (conv_rows_ref, conv_rows),
    )
    copies = copies_of(
        small + ((heads_ref, heads_out), (xz_ref.at[0], in_out), (xproj_ref, xproj_out)), sems
    )
    for copy in copies:
        copy.start()
    for copy in copies[: len(small)]:
        copy.wait()
    me = lax.axis_index("narrow")
    slots = chosen_ref.shape[1]
    row_id = lax.broadcasted_iota(jnp.int32, (8, slots), 0)
    wanted = jnp.full((8, slots), -1, jnp.int32)
    for r in range(rows):
        away = lax.bitwise_xor(lax.div(source[r], rows), lax.axis_index("wide"))
        entry = entry_of(away, size, me)
        wanted = jnp.where(row_id == r, entry * rows + lax.rem(source[r], rows), wanted)
    chosen = lax.broadcasted_iota(jnp.int32, (8, slots), 1) == wanted
    chosen_ref[...] = jnp.where(chosen, 1.0, 0.0)
    live_ref[...] = live_slots(lengths, live_ref.shape[1], me)
    gain_out[...] = gain[...][None]
    taps = conv_rows.shape[0]
    base = conv_b[...]
    for tap in range(taps):
        base = base + conv_w[tap : tap + 1] * conv_rows[tap].astype(F32)
    base_ref[:rows] = base
    base_ref[rows:] = jnp.broadcast_to(conv_w[taps:], base.shape)
    for tap in range(taps - 1):
        new_conv_ref[tap] = conv_rows[tap + 1]
    new_conv_ref[taps - 1] = jnp.zeros_like(conv_rows[0])
    for copy in copies[len(small) :]:
        copy.wait()


def project_in(*refs, size):
    arrived_refs = refs[:size]
    (other_w_ref, chosen_ref, base_ref, gain_ref, heads_w_ref, xproj_ref, in_w_ref, part_ref,
     state_ref, act_ref, normed_ref, channel_ref, routed_ref) = refs[size:]
    rows = act_ref.shape[0]
    arrived = jnp.concatenate(
        [ref[i].astype(F32) for ref in arrived_refs for i in range(ref.shape[0])], axis=0
    ).astype(BF16)
    routed = jnp.dot(chosen_ref[...].astype(BF16), arrived, preferred_element_type=F32)
    routed_ref[...] = routed
    scale = lax.rsqrt(jnp.mean(routed * routed, axis=1, keepdims=True) + EPSILON)
    normed = (routed * scale * gain_ref[...]).astype(BF16)
    normed_ref[...] = normed
    channel_in = dot_nt(normed, in_w_ref[...])[:rows]
    heads = [
        dot_nt(normed, w[...])[:rows].astype(BF16).astype(F32) for w in (heads_w_ref, other_w_ref)
    ]
    channel_ref[...] = channel_in
    conv_out = base_ref[:rows] + base_ref[rows:] * channel_in
    act = conv_out * sigmoid(conv_out)
    act_ref[...] = act
    state = dot_nt(act.astype(BF16), xproj_ref[...])
    state_ref[...] = state
    part_ref[...] = jnp.concatenate([*heads, state], axis=1)


def keep(
    channel_ref, old_conv_ref, kv_ref, ssm_ref, routed_ref, new_conv_ref, new_kv_ref, new_ssm_ref,
    cols_ref, blocks,
):
    rows, cols = cols_ref.shape
    for block in range(blocks.shape[0]):
        blocks[block] = routed_ref[:rows, block * cols : (block + 1) * cols]
    cols_ref[...] = blocks[lax.axis_index("narrow")]
    new_kv_ref[...] = kv_ref[...].astype(BF16)
    new_ssm_ref[...] = ssm_ref[...]
    taps = new_conv_ref.shape[0]
    for tap in range(taps - 1):
        new_conv_ref[tap] = old_conv_ref[tap]
    new_conv_ref[taps - 1] = channel_ref[...].astype(BF16)


def state_step(far_ref, *refs, size):
    states = refs[: size - 1]
    (normed_ref, gate_w_ref, act_ref, dt_w_ref, dt_b_ref, a_log_ref, ssm_ref, skip_ref, out_w_ref,
     part_ref, new_ssm_ref) = refs[size - 1 :]
    state = far_ref[:, far_ref.shape[1] - states[0].shape[1] :]
    for other in states:
        state = state + other[...]
    rows = state.shape[0]
    gate = dot_nt(normed_ref[...], gate_w_ref[1])[:rows]
    rank = dt_w_ref.shape[1]
    depth = a_log_ref.shape[0]
    step = dot_nt(state[:, :rank].astype(BF16), dt_w_ref[...]) + dt_b_ref[...]
    step = jnp.maximum(step, 0.0) + jnp.log1p(jnp.exp(-jnp.abs(step)))
    act = act_ref[...]
    rates = jnp.exp(a_log_ref[...])
    maps = jnp.concatenate(
        [state[:, rank:], jnp.zeros((rows, 128 - 2 * depth), F32)], axis=1
    )
    maps = jnp.concatenate([maps, jnp.zeros((8 - rows, 128), F32)], axis=0).T
    outs = []
    for r in range(rows):
        step_row = step[r : r + 1]
        fresh = jnp.exp(-step_row * rates) * ssm_ref[r] + maps[:depth, r : r + 1] * (
            step_row * act[r : r + 1]
        )
        new_ssm_ref[r] = fresh
        outs.append(jnp.sum(maps[depth : 2 * depth, r : r + 1] * fresh, axis=0, keepdims=True))
    state_out = jnp.concatenate(outs, axis=0) + skip_ref[...] * act
    ssm_heads = (state_out * (gate * sigmoid(gate))).astype(BF16)
    part_ref[...] = jnp.dot(ssm_heads, out_w_ref[...], preferred_element_type=F32).astype(BF16)


def attend(
    near_ref, far_ref, live_ref, keys_ref, values_ref, part_ref, new_kv_ref, held, *, head_width
):
    me = lax.axis_index("narrow")
    rows = held.shape[1]
    for step in range(held.shape[0]):
        piece = far_ref if step & 2 else near_ref
        at = (step & 1) * head_width
        held[lax.bitwise_xor(me, step)] = piece[:, at : at + head_width]
    heads = jnp.concatenate([held[i] for i in range(held.shape[0])], axis=1)
    new_kv_ref[...] = heads[:, QUERY_WIDTH:]
    tall = jnp.concatenate([heads, jnp.zeros((8 - rows, heads.shape[1]), F32)], axis=0)
    tall = jnp.concatenate([tall, jnp.zeros((8, -tall.shape[1] % 128), F32)], axis=1)
    lane = lax.broadcasted_iota(jnp.int32, (8, 128), 1)
    row = lax.broadcasted_iota(jnp.int32, (8, 128), 0)
    first = lane < HEAD_SIZE

    turned = {}

    def twice(at):
        tile = at // 128
        if tile not in turned:
            line = tall[:, tile * 128 : tile * 128 + 128]
            turned[tile] = (line, pltpu.roll(line, HEAD_SIZE, 1))
        line, other = turned[tile]
        return jnp.where(first, line, other) if at % 128 == 0 else jnp.where(first, other, line)

    blocks = -(-rows // 2)
    own_block = [
        jnp.where(row == jnp.where(first, 2 * i, 2 * i + 1), 1.0, 0.0) for i in range(blocks)
    ]
    half = jnp.where(first, HEAD_SIZE ** -0.5, 0.0)
    groups = range(KEY_VALUE_HEADS)
    queries = [[twice(j * HEAD_SIZE) for j in range(g * GROUP, (g + 1) * GROUP)] for g in groups]
    scores = []
    for g in groups:
        spread = jnp.concatenate(
            [
                jnp.concatenate([q * (HEAD_SIZE ** -0.5) * mask for mask in own_block], axis=1)
                for q in queries[g]
            ],
            axis=0,
        ).astype(BF16)
        keys = jnp.concatenate(
            [keys_ref[r, g * HEAD_SIZE : (g + 1) * HEAD_SIZE, :] for r in range(rows)], axis=0
        )
        scores.append(jnp.dot(spread, keys, preferred_element_type=F32))
    new_keys = [twice(QUERY_WIDTH + g * HEAD_SIZE) * half for g in groups]
    own = [
        jnp.sum(
            jnp.concatenate([q * new_keys[g] for q in queries[g]], axis=0), axis=1, keepdims=True
        )
        for g in groups
    ]

    live = jnp.concatenate([live_ref[...]] * GROUP, axis=0) > 0.0
    tops = [
        jnp.maximum(
            jnp.max(jnp.where(live, scores[g], -jnp.inf), axis=1, keepdims=True), own[g]
        )
        for g in groups
    ]
    weights = [
        jnp.where(live, jnp.exp(scores[g] - tops[g]), 0.0).astype(BF16) for g in groups
    ]
    own_here = jnp.where(me == 0, 1.0, 0.0)
    own_weights = [
        jnp.exp(own[g] - tops[g]).astype(BF16).astype(F32) * own_here for g in groups
    ]
    products = []
    for g in groups:
        values = jnp.concatenate(
            [values_ref[r, g * HEAD_SIZE : (g + 1) * HEAD_SIZE, :] for r in range(rows)], axis=0
        )
        products.append(dot_nt(weights[g], values))
    totals = [
        jnp.sum(weights[g].astype(F32), axis=1, keepdims=True) + own_weights[g] for g in groups
    ]
    stats = jnp.zeros((8, 128), F32)
    numers = []
    for g in groups:
        new_value = twice(QUERY_WIDTH + KEY_VALUE_WIDTH + g * HEAD_SIZE)
        for k in range(GROUP):
            j = g * GROUP + k
            at = slice(8 * k, 8 * k + 8)
            folded = products[g][at, :128] * own_block[0]
            for i in range(1, blocks):
                folded = folded + products[g][at, 128 * i : 128 * i + 128] * own_block[i]
            numers.append(
                folded + pltpu.roll(folded, HEAD_SIZE, 1) + own_weights[g][at] * new_value
            )
            stats = jnp.where(lane == j, tops[g][at], stats)
            stats = jnp.where(lane == QUERY_HEADS + j, totals[g][at], stats)
    lines = [
        jnp.where(first, numers[j], numers[j + 1]) for j in range(0, QUERY_HEADS - 1, 2)
    ]
    high = stats.astype(BF16).astype(F32)
    middle = (stats - high).astype(BF16).astype(F32)
    low = stats - high - middle
    lines.append(jnp.where(first, numers[-1], pltpu.roll(high, HEAD_SIZE, 1)))
    lines.append(jnp.where(first, middle, pltpu.roll(low, HEAD_SIZE, 1)))
    part_ref[...] = jnp.concatenate(lines, axis=1)[:rows].astype(BF16)


def project_out(*refs, size):
    pieces = refs[:size]
    (state_ref, spread_ref, w_ref, y_ref, part_ref) = refs[size:]
    rows = y_ref.shape[0]
    stats = [
        functools.reduce(
            jnp.add,
            [
                p[:, QUERY_WIDTH + i * HEAD_SIZE : QUERY_WIDTH + (i + 1) * HEAD_SIZE].astype(F32)
                for i in range(3)
            ],
        )
        for p in pieces
    ]
    tops = [t[:, :QUERY_HEADS] for t in stats]
    totals = [t[:, QUERY_HEADS : 2 * QUERY_HEADS] for t in stats]
    top = functools.reduce(jnp.maximum, tops)
    factors = [jnp.exp(t - top) for t in tops]
    total = functools.reduce(jnp.add, [f * t for f, t in zip(factors, totals)])
    factors = jnp.concatenate([f / total for f in factors], axis=0)
    high = factors.astype(BF16)
    low = (factors - high.astype(F32)).astype(BF16)
    both = jnp.dot(
        jnp.concatenate([high, low], axis=0), spread_ref[...], preferred_element_type=F32
    )
    spread = both[: high.shape[0]] + both[high.shape[0] :]
    merged = functools.reduce(
        jnp.add,
        [spread[i * rows : (i + 1) * rows] * p[:, :QUERY_WIDTH].astype(F32) for i, p in enumerate(pieces)],
    )
    y_attn = dot_nt(merged.astype(BF16), w_ref[...])
    y_ref[...] = y_attn
    square = jnp.sum(y_attn * y_attn, axis=1, keepdims=True)
    high = square.astype(BF16)
    rest = square - high.astype(F32)
    low = rest.astype(BF16)
    lowest = (rest - low.astype(F32)).astype(BF16)
    part_ref[...] = jnp.concatenate(
        [state_ref[...], high, low, lowest, jnp.zeros((rows, part_ref.shape[1] - MODEL_WIDTH - 3), BF16)],
        axis=1,
    )


def finish(*refs, size):
    pieces = refs[:size]
    y_ref, cols_ref, gain_attn_ref, gain_ssm_ref, out_ref, blocks = refs[size:]
    cols = out_ref.shape[1]
    total = functools.reduce(jnp.add, [p[...].astype(F32) for p in pieces])
    square = jnp.sum(total[:, MODEL_WIDTH : MODEL_WIDTH + 3], axis=1, keepdims=True)
    attn_scale = lax.rsqrt(square / MODEL_WIDTH + EPSILON)
    y_ssm = total[:, :MODEL_WIDTH]
    state_scale = lax.rsqrt(jnp.mean(y_ssm * y_ssm, axis=1, keepdims=True) + EPSILON)
    for block in range(blocks.shape[0]):
        blocks[block] = y_ssm[:, block * cols : (block + 1) * cols]
    mixed = 0.5 * (
        y_ref[...] * attn_scale * gain_attn_ref[...]
        + blocks[lax.axis_index("narrow")] * state_scale * gain_ssm_ref[...]
    )
    out_ref[...] = (cols_ref[...] + mixed).astype(BF16)


SMEM = pl.BlockSpec(memory_space=pltpu.SMEM)
VMEM = pl.BlockSpec(memory_space=pltpu.VMEM)


def call(body, scalars, blocks, outs, scratch=(), after=()):
    def run(*refs):
        body(*refs[len(after) :])

    return pl.pallas_call(
        run,
        in_specs=[pl.BlockSpec(memory_space=pl.ANY)] * len(after)
        + [SMEM] * len(scalars)
        + [VMEM] * len(blocks),
        out_specs=[VMEM] * len(outs),
        out_shape=outs,
        scratch_shapes=scratch,
        compiler_params=pltpu.CompilerParams(vmem_limit_bytes=16 * 1024 * 1024),
    )(*after, *scalars, *blocks)


def shards(
    tokens,
    source,
    lengths,
    cached_key_rows,
    cached_value_rows,
    conv_state,
    ssm_state,
    norm_gain,
    query_key_value_weight,
    w_xz,
    conv_weight,
    conv_bias,
    w_xproj,
    w_dt,
    dt_bias,
    a_log,
    skip_d,
    w_attn_out,
    w_ssm_out,
    gain_attn,
    gain_ssm,
):
    rows = tokens.shape[0]
    narrow = lax.axis_size("narrow")
    cols = MODEL_WIDTH // narrow
    head_width = query_key_value_weight.shape[1]
    shape = jax.ShapeDtypeStruct

    wide = lax.axis_size("wide")
    large = (query_key_value_weight.T, w_xproj.T, w_xz.transpose(1, 2, 0))
    small = (source, lengths, norm_gain, conv_weight, conv_bias[None], conv_state.transpose(1, 0, 2))
    slots = rows * entries_of(wide)
    half = large[2].shape[1:]
    pinned = [pltpu.with_memory_space_constraint(a, pltpu.HBM) for a in small + large]
    anywhere = pl.BlockSpec(memory_space=pl.ANY)
    prepared = pl.pallas_call(
        functools.partial(prepare, size=wide),
        in_specs=[anywhere] * len(pinned),
        out_specs=[VMEM] * 8,
        out_shape=[
            pltpu.VMEM((8, slots), F32),
            pltpu.VMEM((8, cached_key_rows.shape[1]), F32),
            pltpu.VMEM((2 * rows, cols), F32),
            pltpu.VMEM(small[5].shape, BF16),
            pltpu.VMEM((1, MODEL_WIDTH), F32),
            pltpu.VMEM(large[0].shape, BF16),
            pltpu.VMEM(large[1].shape, BF16),
            pltpu.VMEM(half, BF16),
        ],
        scratch_shapes=[pltpu.SMEM(a.shape, jnp.int32) for a in small[:2]]
        + [pltpu.VMEM(a.shape, a.dtype) for a in small[2:]]
        + [pltpu.SemaphoreType.DMA((7 + 2 * (PARTS + 1),))],
        compiler_params=pltpu.CompilerParams(vmem_limit_bytes=4 * 1024 * 1024),
    )(*pinned)
    arrived = gather_xor(tokens, "wide", "narrow", prepared[:1])
    other_w = swap(large[0], 1)
    part_width = 2 * head_width + w_xproj.shape[1]
    chosen, live, base, old_conv, *weights = prepared
    part, state, act, normed, channel_in, routed = call(
        functools.partial(project_in, size=len(arrived)),
        (),
        (*arrived, other_w, chosen, base, *weights),
        (
            shape((rows, part_width), F32),
            shape((rows, w_xproj.shape[1]), F32),
            shape((rows, cols), F32),
            shape((8, MODEL_WIDTH), BF16),
            shape((rows, cols), F32),
            shape((8, MODEL_WIDTH), F32),
        ),
    )
    far = swap(part, 2)
    states = [state, swap(state, 1), swap(state, 3)]
    second, key_value = call(
        functools.partial(attend, head_width=head_width),
        (),
        (
            part, far, live, cached_key_rows.transpose(0, 2, 1),
            cached_value_rows.transpose(0, 2, 1),
        ),
        (
            shape((rows, QUERY_WIDTH + 3 * HEAD_SIZE), BF16),
            shape((rows, 2 * KEY_VALUE_WIDTH), F32),
        ),
        (pltpu.VMEM((narrow, rows, head_width), F32),),
    )
    state_part, fresh_ssm = call(
        functools.partial(state_step, size=narrow),
        (),
        (
            far, *states, normed, w_xz.transpose(1, 2, 0), act, w_dt.T, dt_bias[None], a_log, ssm_state, skip_d[None], w_ssm_out,
        ),
        (
            shape((rows, MODEL_WIDTH), BF16),
            shape(ssm_state.shape, F32),
        ),
    )
    pieces = exchange(second, (3, 2, 1))
    spread = (
        lax.broadcasted_iota(jnp.int32, (QUERY_HEADS, QUERY_WIDTH), 1) // HEAD_SIZE
        == lax.broadcasted_iota(jnp.int32, (QUERY_HEADS, QUERY_WIDTH), 0)
    ).astype(BF16)
    y_attn, third = call(
        functools.partial(project_out, size=narrow),
        (),
        (*pieces, state_part, spread, w_attn_out.T),
        (shape((rows, cols), F32), shape((rows, MODEL_WIDTH + 64), BF16)),
    )
    pieces = exchange(third, (3, 2, 1))
    new_conv, new_kv, new_ssm, routed_cols = call(
        keep,
        (),
        (channel_in, old_conv, key_value, fresh_ssm, routed),
        (
            shape(old_conv.shape, BF16),
            shape(key_value.shape, BF16),
            shape(ssm_state.shape, F32),
            shape((rows, cols), F32),
        ),
        (pltpu.VMEM((narrow, rows, cols), F32),),
        after=(third,),
    )
    (out,) = call(
        functools.partial(finish, size=narrow),
        (),
        (*pieces, y_attn, routed_cols, gain_attn[None], gain_ssm[None]),
        (shape((rows, cols), BF16),),
        (pltpu.VMEM((narrow, rows, cols), F32),),
    )
    return (out, new_kv, new_conv.transpose(1, 0, 2), new_ssm)


def solution(mesh):
    placed = (
        P("wide", None),
        P("wide"),
        P("wide"),
        P("wide", "narrow", None),
        P("wide", "narrow", None),
        P("wide", None, "narrow"),
        P("wide", None, "narrow"),
        P(),
        P(None, "narrow"),
        P(None, None, "narrow"),
        P(None, "narrow"),
        P("narrow"),
        P("narrow", None),
        P(None, "narrow"),
        P("narrow"),
        P(None, "narrow"),
        P("narrow"),
        P(None, "narrow"),
        P("narrow", None),
        P("narrow"),
        P("narrow"),
    )
    return jax.shard_map(
        shards,
        mesh=mesh,
        in_specs=placed,
        out_specs=(
            P("wide", "narrow"),
            P("wide", None),
            P("wide", None, "narrow"),
            P("wide", None, "narrow"),
        ),
        check_vma=False,
    )
```

```python
import functools
import jax
import jax.numpy as jnp
from jax import lax
from jax.experimental import pallas as pl
from jax.experimental.pallas import tpu as pltpu
from jax.sharding import PartitionSpec as P

MODEL_WIDTH = 1600
QUERY_HEADS = 25
KEY_VALUE_HEADS = 5
HEAD_SIZE = 64
WINDOW_LENGTH = 1024
GROUP = QUERY_HEADS // KEY_VALUE_HEADS
QUERY_WIDTH = QUERY_HEADS * HEAD_SIZE
KEY_VALUE_WIDTH = KEY_VALUE_HEADS * HEAD_SIZE


EPSILON = 1e-06
PARTS = 4

NT = (((1,), (1,)), ((), ()))
F32 = jnp.float32
BF16 = jnp.bfloat16


def dot_nt(a, b):
    return lax.dot_general(a, b, NT, preferred_element_type=F32)


def sigmoid(v):
    return 1.0 / (1.0 + jnp.exp(-v))


def exchange(part, order):
    return [part] + [swap(part, step) for step in order]


def join(*refs):
    *given, out_ref = refs
    at = 0
    for ref in given:
        out_ref[at : at + ref.shape[0]] = ref[...]
        at += ref.shape[0]


def swap(part, step):
    size = lax.axis_size("narrow")
    assert size == 4
    return lax.ppermute(part, "narrow", [(i, i ^ step) for i in range(size)])


def digits_of(size):
    assert size & (size - 1) == 0
    rounds, done, total = [], 0, size.bit_length() - 1
    while done < total:
        count = 1 if (total - done) % 2 else 2
        rounds.append((done, count))
        done += count
    return rounds


def gather_xor(part, axis, core_axis, beside):
    size, cores = lax.axis_size(axis), lax.axis_size(core_axis)
    blocks = [part[None]]
    rounds = digits_of(size)
    for place, count in rounds:
        held = blocks[0]
        if len(blocks) > 1:
            entries = sum(b.shape[0] for b in blocks)
            (held,) = call(
                join, (), blocks, (jax.ShapeDtypeStruct((entries, *part.shape), part.dtype),), after=beside
            )
            beside = ()
        if count == 2 and place == rounds[-1][0]:

            def fetch(even, odd):
                moves = [
                    (i * cores + c, (i ^ (step << place)) * cores + c)
                    for i in range(size)
                    for c in range(cores)
                    for step in [odd if c % 2 else even]
                    if step
                ]
                return lax.ppermute(held, (axis, core_axis), moves)

            far, near = fetch(3, 2), fetch(0, 1)
            near_swap = lax.ppermute(near, core_axis, [(c, c - 1) for c in range(1, cores, 2)])
            far_swap = lax.ppermute(far, core_axis, [(c, c ^ 1) for c in range(cores)])
            blocks = [held, near, near_swap, far, far_swap]
        else:
            blocks = [held] + [
                lax.ppermute(held, axis, [(i, i ^ (step << place)) for i in range(size)])
                for step in range((1 << count) - 1, 0, -1)
            ]
    return blocks


def entries_of(size):
    rounds = digits_of(size)
    return (5 * size) // 4 if rounds[-1][1] == 2 else size


def entry_of(away, size, core):
    entry, done = jnp.int32(0), 0
    rounds = digits_of(size)
    for place, count in rounds:
        top = (1 << count) - 1
        digit = lax.bitwise_and(lax.shift_right_logical(away, place), top)
        if count == 2 and place == rounds[-1][0]:
            odd = lax.bitwise_and(core, 1)
            near = 2 - odd
            far = jnp.where(digit == 3 - odd, 3, 4)
            block = jnp.where(digit == 0, 0, jnp.where(digit == 1, near, far))
        else:
            block = lax.bitwise_and(top + 1 - digit, top)
        entry = entry + block * (1 << done)
        done += count
    return entry


def cut(rows, count):
    step = -(-rows // (16 * count)) * 16
    return [(at, min(step, rows - at)) for at in range(0, rows, step)]


def copies_of(pairs, sems):
    copies = []
    for origin, to in pairs:
        if len(to.shape) == 2 and to.shape[0] >= 256:
            ranges = [pl.ds(at, size) for at, size in cut(to.shape[0], PARTS)]
            copies += [(origin.at[r], to.at[r]) for r in ranges]
        else:
            copies.append((origin, to))
    return [pltpu.make_async_copy(origin, to, sems.at[i]) for i, (origin, to) in enumerate(copies)]


def live_slots(lengths, span, me):
    row_id = lax.broadcasted_iota(jnp.int32, (8, span), 0)
    slot = lax.broadcasted_iota(jnp.int32, (8, span), 1) + me * span
    length = jnp.zeros((8, span), jnp.int32)
    hole = jnp.zeros((8, span), jnp.int32)
    for r in range(lengths.shape[0]):
        count = lengths[r]
        length = jnp.where(row_id == r, count, length)
        hole = jnp.where(
            row_id == r, jnp.where(count >= WINDOW_LENGTH, lax.rem(count, WINDOW_LENGTH), -1), hole
        )
    return jnp.where((slot < length) & (slot != hole), 1.0, 0.0)


def prepare(
    source_ref, gain_ref, conv_w_ref, conv_b_ref, conv_rows_ref, heads_ref, xproj_ref, xz_ref,
    chosen_ref, base_ref, new_conv_ref, gain_out, heads_out, xproj_out, in_out,
    source, gain, conv_w, conv_b, conv_rows, sems, *, size,
):
    rows = source.shape[0]
    small = (
        (source_ref, source), (gain_ref, gain), (conv_w_ref, conv_w), (conv_b_ref, conv_b),
        (conv_rows_ref, conv_rows),
    )
    copies = copies_of(
        small + ((heads_ref, heads_out), (xz_ref.at[0], in_out), (xproj_ref, xproj_out)), sems
    )
    for copy in copies:
        copy.start()
    for copy in copies[: len(small)]:
        copy.wait()
    me = lax.axis_index("narrow")
    slots = chosen_ref.shape[1]
    row_id = lax.broadcasted_iota(jnp.int32, (8, slots), 0)
    wanted = jnp.full((8, slots), -1, jnp.int32)
    for r in range(rows):
        away = lax.bitwise_xor(lax.div(source[r], rows), lax.axis_index("wide"))
        entry = entry_of(away, size, me)
        wanted = jnp.where(row_id == r, entry * rows + lax.rem(source[r], rows), wanted)
    chosen = lax.broadcasted_iota(jnp.int32, (8, slots), 1) == wanted
    chosen_ref[...] = jnp.where(chosen, 1.0, 0.0)
    gain_out[...] = gain[...][None]
    taps = conv_rows.shape[0]
    base = conv_b[...]
    for tap in range(taps):
        base = base + conv_w[tap : tap + 1] * conv_rows[tap].astype(F32)
    base_ref[:rows] = base
    base_ref[rows:] = jnp.broadcast_to(conv_w[taps:], base.shape)
    for tap in range(taps - 1):
        new_conv_ref[tap] = conv_rows[tap + 1]
    new_conv_ref[taps - 1] = jnp.zeros_like(conv_rows[0])
    for copy in copies[len(small) :]:
        copy.wait()


def mark_live(lengths_ref, live_ref, lengths, sem):
    copy = pltpu.make_async_copy(lengths_ref, lengths, sem)
    copy.start()
    copy.wait()
    live_ref[...] = live_slots(lengths, live_ref.shape[1], lax.axis_index("narrow"))


def project_in(*refs, size):
    arrived_refs = refs[:size]
    (other_w_ref, chosen_ref, base_ref, gain_ref, heads_w_ref, xproj_ref, in_w_ref, part_ref,
     state_ref, act_ref, normed_ref, channel_ref, routed_ref) = refs[size:]
    rows = act_ref.shape[0]
    arrived = jnp.concatenate(
        [ref[i].astype(F32) for ref in arrived_refs for i in range(ref.shape[0])], axis=0
    ).astype(BF16)
    routed = jnp.dot(chosen_ref[...].astype(BF16), arrived, preferred_element_type=F32)
    routed_ref[...] = routed
    scale = lax.rsqrt(jnp.mean(routed * routed, axis=1, keepdims=True) + EPSILON)
    normed = (routed * scale * gain_ref[...]).astype(BF16)
    normed_ref[...] = normed
    channel_in = dot_nt(normed, in_w_ref[...])[:rows]
    heads = [
        dot_nt(normed, w[...])[:rows].astype(BF16).astype(F32) for w in (heads_w_ref, other_w_ref)
    ]
    channel_ref[...] = channel_in
    conv_out = base_ref[:rows] + base_ref[rows:] * channel_in
    act = conv_out * sigmoid(conv_out)
    act_ref[...] = act
    state = dot_nt(act.astype(BF16), xproj_ref[...])
    state_ref[...] = state
    part_ref[...] = jnp.concatenate([*heads, state], axis=1)


def keep(
    channel_ref, old_conv_ref, kv_ref, ssm_ref, routed_ref, new_conv_ref, new_kv_ref, new_ssm_ref,
    cols_ref, blocks,
):
    rows, cols = cols_ref.shape
    for block in range(blocks.shape[0]):
        blocks[block] = routed_ref[:rows, block * cols : (block + 1) * cols]
    cols_ref[...] = blocks[lax.axis_index("narrow")]
    new_kv_ref[...] = kv_ref[...].astype(BF16)
    new_ssm_ref[...] = ssm_ref[...]
    taps = new_conv_ref.shape[0]
    for tap in range(taps - 1):
        new_conv_ref[tap] = old_conv_ref[tap]
    new_conv_ref[taps - 1] = channel_ref[...].astype(BF16)


def state_step(far_ref, *refs, size):
    states = refs[: size - 1]
    (normed_ref, gate_w_ref, act_ref, dt_w_ref, dt_b_ref, a_log_ref, ssm_ref, skip_ref, out_w_ref,
     part_ref, new_ssm_ref) = refs[size - 1 :]
    state = far_ref[:, far_ref.shape[1] - states[0].shape[1] :]
    for other in states:
        state = state + other[...]
    rows = state.shape[0]
    gate = dot_nt(normed_ref[...], gate_w_ref[1])[:rows]
    rank = dt_w_ref.shape[1]
    depth = a_log_ref.shape[0]
    step = dot_nt(state[:, :rank].astype(BF16), dt_w_ref[...]) + dt_b_ref[...]
    step = jnp.maximum(step, 0.0) + jnp.log1p(jnp.exp(-jnp.abs(step)))
    act = act_ref[...]
    rates = jnp.exp(a_log_ref[...])
    maps = jnp.concatenate(
        [state[:, rank:], jnp.zeros((rows, 128 - 2 * depth), F32)], axis=1
    )
    maps = jnp.concatenate([maps, jnp.zeros((8 - rows, 128), F32)], axis=0).T
    outs = []
    for r in range(rows):
        step_row = step[r : r + 1]
        fresh = jnp.exp(-step_row * rates) * ssm_ref[r] + maps[:depth, r : r + 1] * (
            step_row * act[r : r + 1]
        )
        new_ssm_ref[r] = fresh
        outs.append(jnp.sum(maps[depth : 2 * depth, r : r + 1] * fresh, axis=0, keepdims=True))
    state_out = jnp.concatenate(outs, axis=0) + skip_ref[...] * act
    ssm_heads = (state_out * (gate * sigmoid(gate))).astype(BF16)
    part_ref[...] = jnp.dot(ssm_heads, out_w_ref[...], preferred_element_type=F32).astype(BF16)


def attend(
    near_ref, far_ref, live_ref, keys_ref, values_ref, part_ref, new_kv_ref, held, *, head_width
):
    me = lax.axis_index("narrow")
    rows = held.shape[1]
    for step in range(held.shape[0]):
        piece = far_ref if step & 2 else near_ref
        at = (step & 1) * head_width
        held[lax.bitwise_xor(me, step)] = piece[:, at : at + head_width]
    heads = jnp.concatenate([held[i] for i in range(held.shape[0])], axis=1)
    new_kv_ref[...] = heads[:, QUERY_WIDTH:]
    tall = jnp.concatenate([heads, jnp.zeros((8 - rows, heads.shape[1]), F32)], axis=0)
    tall = jnp.concatenate([tall, jnp.zeros((8, -tall.shape[1] % 128), F32)], axis=1)
    lane = lax.broadcasted_iota(jnp.int32, (8, 128), 1)
    row = lax.broadcasted_iota(jnp.int32, (8, 128), 0)
    first = lane < HEAD_SIZE

    turned = {}

    def twice(at):
        tile = at // 128
        if tile not in turned:
            line = tall[:, tile * 128 : tile * 128 + 128]
            turned[tile] = (line, pltpu.roll(line, HEAD_SIZE, 1))
        line, other = turned[tile]
        return jnp.where(first, line, other) if at % 128 == 0 else jnp.where(first, other, line)

    blocks = -(-rows // 2)
    own_block = [
        jnp.where(row == jnp.where(first, 2 * i, 2 * i + 1), 1.0, 0.0) for i in range(blocks)
    ]
    half = jnp.where(first, HEAD_SIZE ** -0.5, 0.0)
    groups = range(KEY_VALUE_HEADS)
    queries = [[twice(j * HEAD_SIZE) for j in range(g * GROUP, (g + 1) * GROUP)] for g in groups]
    scores = []
    for g in groups:
        spread = jnp.concatenate(
            [
                jnp.concatenate([q * (HEAD_SIZE ** -0.5) * mask for mask in own_block], axis=1)
                for q in queries[g]
            ],
            axis=0,
        ).astype(BF16)
        keys = jnp.concatenate(
            [keys_ref[r, g * HEAD_SIZE : (g + 1) * HEAD_SIZE, :] for r in range(rows)], axis=0
        )
        scores.append(jnp.dot(spread, keys, preferred_element_type=F32))
    new_keys = [twice(QUERY_WIDTH + g * HEAD_SIZE) * half for g in groups]
    own = [
        jnp.sum(
            jnp.concatenate([q * new_keys[g] for q in queries[g]], axis=0), axis=1, keepdims=True
        )
        for g in groups
    ]

    live = jnp.concatenate([live_ref[...]] * GROUP, axis=0) > 0.0
    tops = [
        jnp.maximum(
            jnp.max(jnp.where(live, scores[g], -jnp.inf), axis=1, keepdims=True), own[g]
        )
        for g in groups
    ]
    weights = [
        jnp.where(live, jnp.exp(scores[g] - tops[g]), 0.0).astype(BF16) for g in groups
    ]
    own_here = jnp.where(me == 0, 1.0, 0.0)
    own_weights = [
        jnp.exp(own[g] - tops[g]).astype(BF16).astype(F32) * own_here for g in groups
    ]
    products = []
    for g in groups:
        values = jnp.concatenate(
            [values_ref[r, g * HEAD_SIZE : (g + 1) * HEAD_SIZE, :] for r in range(rows)], axis=0
        )
        products.append(dot_nt(weights[g], values))
    totals = [
        jnp.sum(weights[g].astype(F32), axis=1, keepdims=True) + own_weights[g] for g in groups
    ]
    stats = jnp.zeros((8, 128), F32)
    numers = []
    for g in groups:
        new_value = twice(QUERY_WIDTH + KEY_VALUE_WIDTH + g * HEAD_SIZE)
        for k in range(GROUP):
            j = g * GROUP + k
            at = slice(8 * k, 8 * k + 8)
            folded = products[g][at, :128] * own_block[0]
            for i in range(1, blocks):
                folded = folded + products[g][at, 128 * i : 128 * i + 128] * own_block[i]
            numers.append(
                folded + pltpu.roll(folded, HEAD_SIZE, 1) + own_weights[g][at] * new_value
            )
            stats = jnp.where(lane == j, tops[g][at], stats)
            stats = jnp.where(lane == QUERY_HEADS + j, totals[g][at], stats)
    lines = [
        jnp.where(first, numers[j], numers[j + 1]) for j in range(0, QUERY_HEADS - 1, 2)
    ]
    high = stats.astype(BF16).astype(F32)
    middle = (stats - high).astype(BF16).astype(F32)
    low = stats - high - middle
    lines.append(jnp.where(first, numers[-1], pltpu.roll(high, HEAD_SIZE, 1)))
    lines.append(jnp.where(first, middle, pltpu.roll(low, HEAD_SIZE, 1)))
    part_ref[...] = jnp.concatenate(lines, axis=1)[:rows].astype(BF16)


def project_out(*refs, size):
    pieces = refs[:size]
    (state_ref, spread_ref, w_ref, y_ref, part_ref) = refs[size:]
    rows = y_ref.shape[0]
    stats = [
        functools.reduce(
            jnp.add,
            [
                p[:, QUERY_WIDTH + i * HEAD_SIZE : QUERY_WIDTH + (i + 1) * HEAD_SIZE].astype(F32)
                for i in range(3)
            ],
        )
        for p in pieces
    ]
    tops = [t[:, :QUERY_HEADS] for t in stats]
    totals = [t[:, QUERY_HEADS : 2 * QUERY_HEADS] for t in stats]
    top = functools.reduce(jnp.maximum, tops)
    factors = [jnp.exp(t - top) for t in tops]
    total = functools.reduce(jnp.add, [f * t for f, t in zip(factors, totals)])
    factors = jnp.concatenate([f / total for f in factors], axis=0)
    high = factors.astype(BF16)
    low = (factors - high.astype(F32)).astype(BF16)
    both = jnp.dot(
        jnp.concatenate([high, low], axis=0), spread_ref[...], preferred_element_type=F32
    )
    spread = both[: high.shape[0]] + both[high.shape[0] :]
    merged = functools.reduce(
        jnp.add,
        [spread[i * rows : (i + 1) * rows] * p[:, :QUERY_WIDTH].astype(F32) for i, p in enumerate(pieces)],
    )
    y_attn = dot_nt(merged.astype(BF16), w_ref[...])
    y_ref[...] = y_attn
    square = jnp.sum(y_attn * y_attn, axis=1, keepdims=True)
    high = square.astype(BF16)
    rest = square - high.astype(F32)
    low = rest.astype(BF16)
    lowest = (rest - low.astype(F32)).astype(BF16)
    part_ref[...] = jnp.concatenate(
        [state_ref[...], high, low, lowest, jnp.zeros((rows, part_ref.shape[1] - MODEL_WIDTH - 3), BF16)],
        axis=1,
    )


def finish(*refs, size):
    pieces = refs[:size]
    y_ref, cols_ref, gain_attn_ref, gain_ssm_ref, out_ref, blocks = refs[size:]
    cols = out_ref.shape[1]
    total = functools.reduce(jnp.add, [p[...].astype(F32) for p in pieces])
    square = jnp.sum(total[:, MODEL_WIDTH : MODEL_WIDTH + 3], axis=1, keepdims=True)
    attn_scale = lax.rsqrt(square / MODEL_WIDTH + EPSILON)
    y_ssm = total[:, :MODEL_WIDTH]
    state_scale = lax.rsqrt(jnp.mean(y_ssm * y_ssm, axis=1, keepdims=True) + EPSILON)
    for block in range(blocks.shape[0]):
        blocks[block] = y_ssm[:, block * cols : (block + 1) * cols]
    mixed = 0.5 * (
        y_ref[...] * attn_scale * gain_attn_ref[...]
        + blocks[lax.axis_index("narrow")] * state_scale * gain_ssm_ref[...]
    )
    out_ref[...] = (cols_ref[...] + mixed).astype(BF16)


SMEM = pl.BlockSpec(memory_space=pltpu.SMEM)
VMEM = pl.BlockSpec(memory_space=pltpu.VMEM)


def call(body, scalars, blocks, outs, scratch=(), after=()):
    def run(*refs):
        body(*refs[len(after) :])

    return pl.pallas_call(
        run,
        in_specs=[pl.BlockSpec(memory_space=pl.ANY)] * len(after)
        + [SMEM] * len(scalars)
        + [VMEM] * len(blocks),
        out_specs=[VMEM] * len(outs),
        out_shape=outs,
        scratch_shapes=scratch,
        compiler_params=pltpu.CompilerParams(vmem_limit_bytes=16 * 1024 * 1024),
    )(*after, *scalars, *blocks)


def shards(
    tokens,
    source,
    lengths,
    cached_key_rows,
    cached_value_rows,
    conv_state,
    ssm_state,
    norm_gain,
    query_key_value_weight,
    w_xz,
    conv_weight,
    conv_bias,
    w_xproj,
    w_dt,
    dt_bias,
    a_log,
    skip_d,
    w_attn_out,
    w_ssm_out,
    gain_attn,
    gain_ssm,
):
    rows = tokens.shape[0]
    narrow = lax.axis_size("narrow")
    cols = MODEL_WIDTH // narrow
    head_width = query_key_value_weight.shape[1]
    shape = jax.ShapeDtypeStruct

    wide = lax.axis_size("wide")
    large = (query_key_value_weight.T, w_xproj.T, w_xz.transpose(1, 2, 0))
    small = (source, norm_gain, conv_weight, conv_bias[None], conv_state.transpose(1, 0, 2))
    slots = rows * entries_of(wide)
    half = large[2].shape[1:]
    pinned = [pltpu.with_memory_space_constraint(a, pltpu.HBM) for a in small + large]
    anywhere = pl.BlockSpec(memory_space=pl.ANY)
    prepared = pl.pallas_call(
        functools.partial(prepare, size=wide),
        in_specs=[anywhere] * len(pinned),
        out_specs=[VMEM] * 7,
        out_shape=[
            pltpu.VMEM((8, slots), F32),
            pltpu.VMEM((2 * rows, cols), F32),
            pltpu.VMEM(small[4].shape, BF16),
            pltpu.VMEM((1, MODEL_WIDTH), F32),
            pltpu.VMEM(large[0].shape, BF16),
            pltpu.VMEM(large[1].shape, BF16),
            pltpu.VMEM(half, BF16),
        ],
        scratch_shapes=[pltpu.SMEM(a.shape, jnp.int32) for a in small[:1]]
        + [pltpu.VMEM(a.shape, a.dtype) for a in small[1:]]
        + [pltpu.SemaphoreType.DMA((7 + 2 * (PARTS + 1),))],
        compiler_params=pltpu.CompilerParams(vmem_limit_bytes=4 * 1024 * 1024),
    )(*pinned)
    arrived = gather_xor(tokens, "wide", "narrow", prepared[:1])
    other_w = swap(large[0], 1)
    part_width = 2 * head_width + w_xproj.shape[1]
    chosen, base, old_conv, *weights = prepared
    part, state, act, normed, channel_in, routed = call(
        functools.partial(project_in, size=len(arrived)),
        (),
        (*arrived, other_w, chosen, base, *weights),
        (
            shape((rows, part_width), F32),
            shape((rows, w_xproj.shape[1]), F32),
            shape((rows, cols), F32),
            shape((8, MODEL_WIDTH), BF16),
            shape((rows, cols), F32),
            shape((8, MODEL_WIDTH), F32),
        ),
    )
    far = swap(part, 2)

    def mark(after_ref, *refs):
        mark_live(*refs)

    live = pl.pallas_call(
        mark,
        in_specs=[anywhere] * 2,
        out_specs=VMEM,
        out_shape=pltpu.VMEM((8, cached_key_rows.shape[1]), F32),
        scratch_shapes=[pltpu.SMEM(lengths.shape, jnp.int32), pltpu.SemaphoreType.DMA(())],
        compiler_params=pltpu.CompilerParams(vmem_limit_bytes=4 * 1024 * 1024),
    )(normed, pltpu.with_memory_space_constraint(lengths, pltpu.HBM))
    states = [state, swap(state, 1), swap(state, 3)]
    second, key_value = call(
        functools.partial(attend, head_width=head_width),
        (),
        (
            part, far, live, cached_key_rows.transpose(0, 2, 1),
            cached_value_rows.transpose(0, 2, 1),
        ),
        (
            shape((rows, QUERY_WIDTH + 3 * HEAD_SIZE), BF16),
            shape((rows, 2 * KEY_VALUE_WIDTH), F32),
        ),
        (pltpu.VMEM((narrow, rows, head_width), F32),),
    )
    state_part, fresh_ssm = call(
        functools.partial(state_step, size=narrow),
        (),
        (
            far, *states, normed, w_xz.transpose(1, 2, 0), act, w_dt.T, dt_bias[None], a_log, ssm_state, skip_d[None], w_ssm_out,
        ),
        (
            shape((rows, MODEL_WIDTH), BF16),
            shape(ssm_state.shape, F32),
        ),
    )
    pieces = exchange(second, (3, 2, 1))
    spread = (
        lax.broadcasted_iota(jnp.int32, (QUERY_HEADS, QUERY_WIDTH), 1) // HEAD_SIZE
        == lax.broadcasted_iota(jnp.int32, (QUERY_HEADS, QUERY_WIDTH), 0)
    ).astype(BF16)
    y_attn, third = call(
        functools.partial(project_out, size=narrow),
        (),
        (*pieces, state_part, spread, w_attn_out.T),
        (shape((rows, cols), F32), shape((rows, MODEL_WIDTH + 64), BF16)),
    )
    pieces = exchange(third, (3, 2, 1))
    new_conv, new_kv, new_ssm, routed_cols = call(
        keep,
        (),
        (channel_in, old_conv, key_value, fresh_ssm, routed),
        (
            shape(old_conv.shape, BF16),
            shape(key_value.shape, BF16),
            shape(ssm_state.shape, F32),
            shape((rows, cols), F32),
        ),
        (pltpu.VMEM((narrow, rows, cols), F32),),
        after=(third,),
    )
    (out,) = call(
        functools.partial(finish, size=narrow),
        (),
        (*pieces, y_attn, routed_cols, gain_attn[None], gain_ssm[None]),
        (shape((rows, cols), BF16),),
        (pltpu.VMEM((narrow, rows, cols), F32),),
    )
    return (out, new_kv, new_conv.transpose(1, 0, 2), new_ssm)


def solution(mesh):
    placed = (
        P("wide", None),
        P("wide"),
        P("wide"),
        P("wide", "narrow", None),
        P("wide", "narrow", None),
        P("wide", None, "narrow"),
        P("wide", None, "narrow"),
        P(),
        P(None, "narrow"),
        P(None, None, "narrow"),
        P(None, "narrow"),
        P("narrow"),
        P("narrow", None),
        P(None, "narrow"),
        P("narrow"),
        P(None, "narrow"),
        P("narrow"),
        P(None, "narrow"),
        P("narrow", None),
        P("narrow"),
        P("narrow"),
    )
    return jax.shard_map(
        shards,
        mesh=mesh,
        in_specs=placed,
        out_specs=(
            P("wide", "narrow"),
            P("wide", None),
            P("wide", None, "narrow"),
            P("wide", None, "narrow"),
        ),
        check_vma=False,
    )
```
